256 devices in a mesh: ep: 32 (over y, x, core), dp: 8 (over z).
Axes of the slice: x: 4, y: 4, z: 8, core: 2. Of those that a mesh axis runs over, the one named last changes fastest.
Arguments:
- out_grad: bfloat16 [8, 4096, 2048], P('dp', 'ep'), may hold values from -6 to 6
- gates: bfloat16 [8, 4096, 8], P('dp', 'ep'), may hold values from 0.019897461 to 0.5
- routes: int32 [8, 4096, 8], P('dp', 'ep'), may hold values from 0 to 127, all different within a row; in each aligned block of 128 rows (0 to 127, 128 to 255, ..., all dimensions but the last counted through in order) at most 12 rows name the same one
- expert_slot: int32 [128], replicated, may hold values from 0 to 127, each once
- hidden_saved: bfloat16 [8, 128, 32, 12, 768], P('dp', 'ep'), may hold values from -6 to 6
- w_down: bfloat16 [2048, 98304], P('dp', 'ep'), may hold values from -0.21875 to 0.21875
Outputs:
- hidden_grad: bfloat16 [8, 128, 32, 12, 768], P('dp', 'ep')
- gate_grad: float32 [8, 4096, 8], P('dp', 'ep')
- weight_grad: float32 [2048, 98304], P('dp', 'ep')
The draws below stay inside these ranges and needn't reach their ends.
Inputs may be any that keep to these rules, and one draw needn't show every extreme that they name: `routes`: the rows of one device name no expert more than 12 times, and every expert is named by some row. `expert_slot`: each slot once.
All inputs are finite; a program needn't handle non-finite values.
Results may differ from the reference program's by a relative error of at most 0.012.
Values may be sent and summed in bfloat16 or wider, within the bound.
A program may use at most 128 MiB of HBM per device.

```python
import math
import jax
import jax.numpy as jnp
import numpy as np
from jax import lax

D = 2048
H = 768
TOPK = 8
TOK_DEV = 128
EXPERTS = 128
CAP = 12
GROUP_TOK = 4096
N_EP = 32
N_DP = 8


def block_scale(rng, shape, split, smallest, largest):
    loudness = 1.0
    for position, parts in split:
        steps = jax.random.uniform(jax.random.fold_in(jax.random.fold_in(rng, 6), position), (parts,), jnp.float32, smallest / len(split), largest / len(split))
        loudness = loudness * jnp.repeat(jnp.exp(steps), shape[position] // parts).reshape((-1,) + (1,) * (len(shape) - 1 - position))
    return loudness


def routed_block(stream_key, own, number, rows, count, top, reach, lean):
    ranking = jax.random.permutation(stream_key, count)
    heavy_load, common = load_shares(count, rows * top, reach, lean, True), load_shares(count, rows * top, reach, lean, False)
    places = jnp.arange(count)

    def named(lengths, rotation):
        used = int((lengths > 0).sum())
        fixed = max(1, used // 4)
        passed = fixed + (places - fixed + rotation * (used - fixed)) % max(1, count - fixed)
        return jnp.zeros((count,), jnp.int32).at[ranking[jnp.where(places < fixed, places, passed)]].set(jnp.asarray(lengths, jnp.int32))

    lengths = jnp.where(number % 4 == 0, named(heavy_load, number // 4), named(common, number - number // 4 - 1))
    mixed = jax.random.permutation(jax.random.fold_in(own, 3), count)
    source_of, taker = mixed[0:count // 2 * 2:2], mixed[1:count // 2 * 2:2]
    slack = jnp.minimum(lengths[source_of] - 1, reach - lengths[taker]) // 2
    slack = jnp.where((source_of == ranking[0]) | (taker == ranking[0]) | (lengths[taker] == 0), 0, jnp.maximum(slack, 0))
    passed = jax.random.randint(jax.random.fold_in(own, 4), (count // 2,), 0, 1 << 20) % (slack + 1)
    lengths = lengths.at[source_of].add(-passed).at[taker].add(passed)
    members = jnp.searchsorted(jnp.cumsum(lengths), jnp.arange(rows * top), side="right").astype(jnp.int32)
    listing = members.reshape(top, rows).T
    listing = listing[jax.random.permutation(jax.random.fold_in(own, 1), rows)]
    rotation = jax.random.randint(jax.random.fold_in(own, 2), (rows, 1), 0, top)
    return jnp.take_along_axis(listing, (jnp.arange(top)[None, :] + rotation) % top, axis=1)


def load_shares(number_of, total, most, slope, full):
    loads = [(1 << 20) // math.isqrt(standing ** slope) + 1 for standing in range(1, number_of + 1)]
    largest = most if full else min(most, max(-(-total // number_of), total * loads[0] // sum(loads)))
    least = 1 if total - largest >= number_of - 1 else 0
    counts, spare = [largest] + [least] * (number_of - 1), total - largest - least * (number_of - 1)
    while spare > 0:
        candidates = [i for i in range(1, number_of) if counts[i] < largest] or [i for i in range(1, number_of) if counts[i] < most]
        whole, budget = sum([loads[i] for i in candidates]), spare
        for i in candidates:
            extra = min(most - counts[i], max(1, budget * loads[i] // whole), spare)
            counts[i] = counts[i] + extra
            spare = spare - extra
    return np.array(counts)


def centred(rng, shape, spread, bound, pieces=(), kind=jnp.bfloat16):
    drawn = jax.random.normal(rng, shape, jnp.float32) * spread
    if len(pieces) > 0:
        drawn = block_scale(rng, shape, pieces, -0.22, 0.18) * drawn
    return jnp.clip(drawn, min=-bound, max=bound).astype(kind)


def setup_inputs(seed: int = 0) -> dict:
    splits = jax.random.split(jax.random.key(seed), 7)
    out_grad = centred(splits[0], (N_DP, GROUP_TOK, D), 1.0, 6.0, ((0, 8), (1, 32)))
    gates = jnp.clip(0.019897461 + 0.48010254 * jax.random.uniform(splits[1], (N_DP, GROUP_TOK, TOPK), jnp.float32) ** block_scale(splits[1], (N_DP, GROUP_TOK, TOPK), ((0, 8), (1, 32)), -0.2, 0.2), 0.019897461, 0.5).astype(jnp.bfloat16)
    routes_keys = jax.random.split(jax.random.fold_in(splits[2], 1), N_DP * GROUP_TOK // TOK_DEV)
    routes_turns = jax.random.permutation(jax.random.fold_in(splits[2], 3), N_DP * GROUP_TOK // TOK_DEV)
    routes = jax.vmap(lambda own, number: routed_block(jax.random.fold_in(splits[2], 2), own, number, TOK_DEV, EXPERTS, TOPK, CAP, 2))(routes_keys, routes_turns).reshape((N_DP, GROUP_TOK, TOPK))
    expert_slot = jax.random.permutation(splits[3], EXPERTS).astype(jnp.int32)
    hidden_saved = centred(splits[4], (N_DP, EXPERTS, N_EP, CAP, H), 1.0, 6.0, ((0, 8), (1, 32)))
    w_down = centred(splits[5], (D, EXPERTS * H), H ** -0.5, 0.21875, ((0, 8), (1, 32)))
    return {"out_grad": out_grad, "gates": gates, "routes": routes, "expert_slot": expert_slot, "hidden_saved": hidden_saved, "w_down": w_down}


def group_pass(weight_sum, items, expert_slot, w_full):
    out_rows, gate_rows, route_rows, saved = items
    flat_ids = route_rows.reshape(N_EP, TOK_DEV * TOPK)
    onehot = (flat_ids[:, :, None] == jnp.arange(EXPERTS, dtype=jnp.int32)[None, None, :]).astype(jnp.int32)
    slot_ids = jnp.sum(onehot * expert_slot[None, None, :], axis=2).astype(jnp.int32)
    ranks = jnp.sum(onehot * (jnp.cumsum(onehot, axis=1) - 1), axis=2).astype(jnp.int32)
    target = (slot_ids * CAP + ranks).astype(jnp.int32)
    sources = jnp.broadcast_to(jnp.arange(N_EP, dtype=jnp.int32)[:, None], target.shape)
    rows = jnp.repeat(out_rows.reshape(N_EP, TOK_DEV, D), TOPK, axis=1)
    gate_vals = gate_rows.reshape(N_EP, TOK_DEV * TOPK)
    sent = jnp.zeros((N_EP, EXPERTS * CAP, D), jnp.bfloat16).at[sources, target].set(rows)
    sent_gates = jnp.zeros((N_EP, EXPERTS * CAP), jnp.bfloat16).at[sources, target].set(gate_vals)
    sent = sent.reshape(N_EP, EXPERTS, CAP, D)
    gates_qsc = sent_gates.reshape(N_EP, EXPERTS, CAP).transpose(1, 0, 2).astype(jnp.float32)
    u = jnp.einsum('sqcd,dqj->qscj', sent.astype(jnp.float32), w_full.astype(jnp.float32))
    hidden_grad = (gates_qsc[..., None] * u).astype(jnp.bfloat16)
    slot_grad = jnp.sum(saved.astype(jnp.float32) * u, axis=3)
    by_source = slot_grad.transpose(1, 0, 2).reshape(N_EP, EXPERTS * CAP)
    gate_grad = jnp.take_along_axis(by_source, target, axis=1).reshape(N_EP * TOK_DEV, TOPK)
    scaled = (gates_qsc[..., None] * saved.astype(jnp.float32)).astype(jnp.bfloat16)
    partial_value = jnp.einsum('sqcd,qscj->dqj', sent.astype(jnp.float32), scaled.astype(jnp.float32)).astype(jnp.bfloat16)
    weight_sum = weight_sum + partial_value.reshape(D, EXPERTS * H).astype(jnp.float32)
    return weight_sum, (hidden_grad, gate_grad)


def reference(out_grad, gates, routes, expert_slot, hidden_saved, w_down):
    w_full = w_down.reshape(D, EXPERTS, H)
    start = jnp.zeros((D, EXPERTS * H), jnp.float32)

    def step(carry, items):
        return group_pass(carry, items, expert_slot, w_full)

    weight_grad, (hidden_grad, gate_grad) = lax.scan(step, start, (out_grad, gates, routes, hidden_saved))
    return hidden_grad, gate_grad, weight_grad
```

```python
import jax
import jax.numpy as jnp
from jax import lax
from jax.experimental import pallas as pl
from jax.experimental.pallas import tpu as pltpu
from jax.sharding import PartitionSpec as P

BF = jnp.bfloat16
F32 = jnp.float32
MESH = pl.DeviceIdType.MESH
NX, NY, NC, NZ = 4, 4, 2, 8
NE = NX * NY * NC
TOK, D, TOPK = 128, 2048, 8
EXPERTS, LOCAL, CAP, HID = 128, 4, 12, 768
DS = D // NZ
EXT = D + 2 * EXPERTS
ROWS = CAP * NE
SUB = DS // 4
STEPS = NZ - 1


def kernel(
    w_ref, og_ref, rt_ref, gt_ref, es_ref, hs_ref,
    hg_ref, gg_ref, wg_ref,
    T, W, X, G, S, H, R, Fst, Tm, SG, O, Pb, meta,
    ag_s, ag_r, rs_s, rs_r, tk_s, tk_r, sg_s, sg_r, loc,
):
    ep, z = lax.axis_index("ep"), lax.axis_index("dp")
    c, x, y = ep % NC, (ep // NC) % NX, ep // (NC * NX)

    def at(yy, xx, cc):
        return ((yy * NX + xx) * NC + cc, z)

    x_up, x_dn = (x + 1) % NX, (x + NX - 1) % NX
    y_up, y_dn = (y + 1) % NY, (y + NY - 1) % NY
    z_up, z_dn = (ep, (z + 1) % NZ), (ep, (z + NZ - 1) % NZ)
    to_xu, to_xd, to_yu, to_yd = at(y, x_up, c), at(y, x_dn, c), at(y_up, x, c), at(y_dn, x, c)
    sibling = at(y, x, 1 - c)

    barrier = pltpu.get_barrier_semaphore()
    for other in (z_up, z_dn, to_xu, to_xd, to_yu, to_yd, sibling):
        pl.semaphore_signal(barrier, inc=1, device_id=other, device_id_type=MESH)
    pl.semaphore_wait(barrier, 7)

    def ag(t, i):
        rows = pl.ds(i * SUB, SUB)
        owner = (z + NZ - t) % NZ if i < 2 else (z + t) % NZ
        return pltpu.make_async_remote_copy(
            src_ref=w_ref.at[rows] if t == 0 else W.at[owner, rows],
            dst_ref=W.at[owner, rows],
            send_sem=ag_s.at[t, i],
            recv_sem=ag_r.at[t, i],
            device_id=z_up if i < 2 else z_dn,
            device_id_type=MESH,
        )

    def ag_next(t, streams):
        for i in streams:
            ag(t, i).wait_recv()
            ag(t + 1, i).start()

    for i in (0, 2, 1, 3):
        ag(0, i).start()
    own_tokens = pltpu.make_async_copy(og_ref, T.at[c, y, x, :, pl.ds(0, D)], loc.at[0])
    own_tokens.start()
    own_saved = pltpu.make_async_copy(hs_ref, H, loc.at[1])
    own_saved.start()
    own_w = pltpu.make_async_copy(w_ref, W.at[z], loc.at[2])
    own_w.start()

    io0 = lax.broadcasted_iota(jnp.int32, (EXPERTS, TOK), 0)
    io1 = lax.broadcasted_iota(jnp.int32, (EXPERTS, TOK), 1)
    es = es_ref[...]
    to_slot = (io0 == es).astype(F32).astype(BF)
    slot_of = jnp.transpose(jnp.broadcast_to(es.astype(F32), (EXPERTS, EXPERTS)))
    named = jnp.zeros((EXPERTS, TOK), F32)
    weight = jnp.zeros((EXPERTS, TOK), F32)
    for k in range(TOPK):
        hit = (io0 == rt_ref[k : k + 1, :]).astype(F32)
        named = named + hit
        weight = weight + hit * gt_ref[k : k + 1, :].astype(F32)
        meta[k : k + 1, :] = jnp.sum(hit * slot_of, axis=0, keepdims=True)
    earlier = (io0 < io1).astype(F32).astype(BF)
    rank = jnp.dot(named.astype(BF), earlier, preferred_element_type=F32)
    for k in range(TOPK):
        hit = (io0 == rt_ref[k : k + 1, :]).astype(F32)
        meta[TOPK + k : TOPK + k + 1, :] = jnp.sum(hit * rank, axis=0, keepdims=True)
    ranks = jnp.dot(to_slot, ((rank + 1.0) * named).astype(BF), preferred_element_type=F32)
    gates = jnp.dot(to_slot, weight.astype(BF), preferred_element_type=F32)
    T[c, y, x, :, D : D + EXPERTS] = ranks.astype(BF)
    T[c, y, x, :, D + EXPERTS : EXT] = jnp.transpose(gates).astype(BF)
    own_tokens.wait()

    half = TOK // 2
    up_rows, dn_rows = pl.ds(0, half), pl.ds(half, half)
    quarter = [pl.ds(i * half // 2, half // 2) for i in range(4)]

    def tk(n, ref, other):
        return pltpu.make_async_remote_copy(
            src_ref=ref,
            dst_ref=ref,
            send_sem=tk_s.at[n],
            recv_sem=tk_r.at[n],
            device_id=other,
            device_id_type=MESH,
        )

    every = pl.ds(0, 4)
    tokens = [
        [
            tk(0, T.at[c, y, x, up_rows], to_xu),
            tk(1, T.at[c, y, x, up_rows], to_xd),
            tk(2, T.at[c, y, x, dn_rows], to_yu),
            tk(3, T.at[c, y, x, dn_rows], to_yd),
        ],
        [
            tk(4, T.at[c, y, x_dn, quarter[0]], to_xu),
            tk(5, T.at[c, y, x_up, quarter[1]], to_xd),
            tk(6, T.at[c, y_dn, x, quarter[2]], to_yu),
            tk(7, T.at[c, y_up, x, quarter[3]], to_yd),
        ],
        [
            tk(8, T.at[c, y, every, up_rows], to_yu),
            tk(9, T.at[c, y, every, up_rows], to_yd),
            tk(10, T.at[c, every, x, dn_rows], to_xu),
            tk(11, T.at[c, every, x, dn_rows], to_xd),
        ],
        [
            tk(12, T.at[c, y_dn, every, quarter[0]], to_yu),
            tk(13, T.at[c, y_up, every, quarter[1]], to_yd),
            tk(14, T.at[c, every, x_dn, quarter[2]], to_xu),
            tk(15, T.at[c, every, x_up, quarter[3]], to_xd),
        ],
        [tk(16, T.at[c, pl.ds(0, 2)], sibling), tk(17, T.at[c, pl.ds(2, 2)], sibling)],
    ]

    def phase(n):
        if n > 0:
            for copy in tokens[n - 1]:
                copy.wait_recv()
        for copy in tokens[n]:
            copy.start()

    phase(0)
    ag_next(0, (0, 2))
    phase(1)
    ag_next(0, (1, 3))
    phase(2)
    ag_next(1, (0, 2))
    ag_next(1, (1, 3))
    ag_next(2, (0, 2))
    phase(3)
    ag_next(2, (1, 3))
    ag_next(3, (0, 2))
    phase(4)
    ag_next(3, (1, 3))
    ag_next(4, (0, 2))
    own_saved.wait()
    tokens[4][0].wait_recv()
    ag_next(4, (1, 3))

    group = ROWS // 2
    io_row = lax.broadcasted_iota(jnp.int32, (group, TOK), 0).astype(F32)
    io16 = lax.broadcasted_iota(jnp.int32, (16, TOK), 0)
    first = pl.multiple_of((ep // 4) * 16, 16)
    wide = 256

    def unit(u, carry):
        a, l = u // LOCAL, u % LOCAL

        @pl.when(u == 2)
        def _():
            ag_next(5, (0, 2))

        @pl.when(u == 4)
        def _():
            tokens[4][1].wait_recv()
            ag_next(5, (1, 3))

        for block in range(16):
            cc, yy, xx = block // 8, (block // 4) % 2, block % 4
            sixteen = T[cc, 2 * a + yy, xx, pl.ds(first, 16), D : D + EXPERTS].astype(F32)
            v = jnp.sum(
                jnp.where(io16 == (ep % 4) * 4 + l, sixteen, 0.0), axis=0, keepdims=True
            )
            source = (yy * NX + xx) * NC + cc
            v = jnp.where(v > 0.5, 16.0 * v + (source - 16.0), -1.0)
            Pb[:, block * TOK : (block + 1) * TOK] = jnp.where(io_row == v, 1.0, 0.0).astype(BF)

        def pick(columns):
            both = [
                jnp.dot(
                    Pb[:, cc * 1024 : (cc + 1) * 1024],
                    T[cc, pl.ds(2 * a, 2), :, :, columns].reshape(1024, wide),
                    preferred_element_type=F32,
                )
                for cc in range(2)
            ]
            return both[0] + both[1]

        here = pl.ds(pl.multiple_of(a * 16, 16), 16)

        def tile(n, carry):
            columns = pl.ds(pl.multiple_of(n * wide, wide), wide)
            X[l, :, here, columns] = pick(columns).astype(BF).reshape(CAP, 16, wide)
            return carry

        lax.fori_loop(0, D // wide, tile, 0)
        last = pick(slice(D, EXT))
        lane = lax.broadcasted_iota(jnp.int32, (group, wide), 1)
        gate = jnp.sum(
            jnp.where(lane == EXPERTS + ep * LOCAL + l, last, 0.0), axis=1, keepdims=True
        )
        G[l, :, here, :] = jnp.broadcast_to(gate, (group, 128)).reshape(CAP, 16, 128)
        return carry

    lax.fori_loop(0, 2 * LOCAL, unit, 0)

    def scale(l, carry):
        gate = G[l].reshape(ROWS, 128)
        for n in range(HID // 128):
            columns = slice(n * 128, (n + 1) * 128)
            S[l, :, columns] = (gate * H[l, :, columns].astype(F32)).astype(BF)
        return carry

    lax.fori_loop(0, LOCAL, scale, 0)

    def terms(t, out):
        def expert(l, carry):
            owner = jnp.where(l < 2, (z + 2 * NZ - 1 - t) % NZ, (z + 1 + t) % NZ)
            lhs = X[l, :, :, pl.ds(pl.multiple_of(owner * DS, DS), DS)].reshape(ROWS, DS)
            for n in range(HID // wide):
                columns = slice(n * wide, (n + 1) * wide)
                out[l, :, columns] = lax.dot_general(
                    lhs, S[l, :, columns], (((0,), (0,)), ((), ())), preferred_element_type=F32
                ).astype(BF)
            return carry

        lax.fori_loop(0, LOCAL, expert, 0)

    def rs(t, l, src):
        return pltpu.make_async_remote_copy(
            src_ref=src,
            dst_ref=R.at[t, l],
            send_sem=rs_s.at[t, l],
            recv_sem=rs_r.at[t, l],
            device_id=z_up if l < 2 else z_dn,
            device_id_type=MESH,
        )

    order = (0, 2, 1, 3)
    terms(0, Fst)
    for l in order:
        rs(0, l, Fst.at[l]).start()
    terms(1, Tm)

    def upstream(l, carry):
        slot = jnp.zeros((ROWS, 1), F32)
        gate = jnp.concatenate([G[l].reshape(ROWS, 128)] * (wide // 128), axis=1)
        for n in range(HID // wide):
            columns = slice(n * wide, (n + 1) * wide)
            weights = W[:, :, pl.ds(pl.multiple_of(l * HID + n * wide, wide), wide)]
            u = jnp.dot(
                X[l].reshape(ROWS, D), weights.reshape(D, wide), preferred_element_type=F32
            )
            slot = slot + jnp.sum(H[l, :, columns].astype(F32) * u, axis=1, keepdims=True)
            H[l, :, columns] = (gate * u).astype(BF)
        lane = lax.broadcasted_iota(jnp.int32, (NE, 128), 1)
        mine = SG[c, y, x]
        for s in range(CAP):
            mine = jnp.where(lane == l * 16 + s, slot[s * NE : (s + 1) * NE, :], mine)
        SG[c, y, x] = mine
        return carry

    out_hidden = pltpu.make_async_copy(H, hg_ref, loc.at[3])

    def sg(n, ref, other):
        return pltpu.make_async_remote_copy(
            src_ref=ref,
            dst_ref=ref,
            send_sem=sg_s.at[n],
            recv_sem=sg_r.at[n],
            device_id=other,
            device_id_type=MESH,
        )

    slots = [
        [sg(0, SG.at[c, y, x], to_xu), sg(1, SG.at[c, y, x], to_xd)],
        [sg(2, SG.at[c, y, x_dn], to_xu)],
        [sg(3, SG.at[c, y], to_yu), sg(4, SG.at[c, y], to_yd)],
        [sg(5, SG.at[c, y_dn], to_yu)],
        [sg(6, SG.at[c], sibling)],
    ]

    def pass_on(n):
        if n > 0:
            for copy in slots[n - 1]:
                copy.wait_recv()
        for copy in slots[n]:
            copy.start()

    SG[c, y, x] = jnp.zeros((NE, 128), F32)

    def step(t, carry):
        for l in order:
            rs(t - 1, l, R.at[t - 1, l]).wait_recv()
            R[t - 1, l] = (R[t - 1, l].astype(F32) + Tm[l].astype(F32)).astype(BF)
            rs(t, l, R.at[t - 1, l]).start()
        terms(t + 1, Tm)

        @pl.when(t == 1)
        def _():
            for i in range(4):
                ag(STEPS - 1, i).wait_recv()
            own_w.wait()

        @pl.when(t <= 2)
        def _():
            lax.fori_loop(2 * t - 2, 2 * t, upstream, 0)

        @pl.when(t == 3)
        def _():
            out_hidden.start()
            pass_on(0)

        @pl.when(t == 4)
        def _():
            pass_on(1)

        @pl.when(t == 5)
        def _():
            pass_on(2)

        @pl.when(t == 6)
        def _():
            pass_on(3)

        return carry

    lax.fori_loop(1, STEPS, step, 0)
    pass_on(4)
    slots[4][0].wait_recv()

    row = lax.broadcasted_iota(jnp.int32, (NE, NE, 128), 1)
    by_dev = jnp.sum(jnp.where(row == ep, SG[...].reshape(NE, NE, 128), 0.0), axis=1)
    high = by_dev.astype(BF)
    low = (by_dev - high.astype(F32)).astype(BF)
    io_dev = lax.broadcasted_iota(jnp.int32, (NE, TOK), 0)
    io_in = lax.broadcasted_iota(jnp.int32, (128, TOK), 0)
    for k in range(TOPK):
        q = meta[k : k + 1, :].astype(jnp.int32)
        r = meta[TOPK + k : TOPK + k + 1, :].astype(jnp.int32)
        device = lax.shift_right_logical(q, 2)
        place = lax.bitwise_and(device, 1) * 16 + lax.shift_right_logical(device, 1)
        pickers = (io_dev == place).astype(F32).astype(BF)
        found = sum(
            lax.dot_general(part, pickers, (((0,), (0,)), ((), ())), preferred_element_type=F32)
            for part in (high, low)
        )
        inside = lax.bitwise_and(q, 3) * 16 + r
        gg_ref[k : k + 1, :] = jnp.sum(
            jnp.where(io_in == inside, found, 0.0), axis=0, keepdims=True
        )

    outs = []
    for l in order:
        rs(STEPS - 1, l, R.at[STEPS - 1, l]).wait_recv()
        O[l] = R[STEPS - 1, l].astype(F32) + Tm[l].astype(F32)
        copy = pltpu.make_async_copy(O.at[l], wg_ref.at[:, pl.ds(l * HID, HID)], loc.at[4 + l])
        copy.start()
        outs.append(copy)

    for t in range(STEPS):
        for i in range(4):
            ag(t, i).wait_send()
            rs(t, i, Fst.at[i]).wait_send()
    for copies in tokens + slots:
        for copy in copies:
            copy.wait_send()
    out_hidden.wait()
    for copy in outs:
        copy.wait()


def local(out_grad, gates, routes, expert_slot, hidden_saved, w_down):
    hbm, vmem = pl.BlockSpec(memory_space=pl.ANY), pl.BlockSpec(memory_space=pltpu.VMEM)
    dma = pltpu.SemaphoreType.DMA
    saved = hidden_saved[0].transpose(0, 2, 1, 3).reshape(LOCAL, ROWS, HID)
    hidden_grad, gate_grad, weight_grad = pl.pallas_call(
        kernel,
        out_shape=(
            jax.ShapeDtypeStruct((LOCAL, ROWS, HID), BF),
            jax.ShapeDtypeStruct((TOPK, TOK), F32),
            jax.ShapeDtypeStruct((DS, LOCAL * HID), F32),
        ),
        in_specs=[hbm, hbm, vmem, vmem, vmem, hbm],
        out_specs=(hbm, vmem, hbm),
        scratch_shapes=[
            pltpu.VMEM((NC, NY, NX, TOK, EXT), BF),
            pltpu.VMEM((NZ, DS, LOCAL * HID), BF),
            pltpu.VMEM((LOCAL, CAP, NE, D), BF),
            pltpu.VMEM((LOCAL, CAP, NE, 128), F32),
            pltpu.VMEM((LOCAL, ROWS, HID), BF),
            pltpu.VMEM((LOCAL, ROWS, HID), BF),
            pltpu.VMEM((STEPS, LOCAL, DS, HID), BF),
            pltpu.VMEM((LOCAL, DS, HID), BF),
            pltpu.VMEM((LOCAL, DS, HID), BF),
            pltpu.VMEM((NC, NY, NX, NE, 128), F32),
            pltpu.VMEM((LOCAL, DS, HID), F32),
            pltpu.VMEM((ROWS // 2, 16 * TOK), BF),
            pltpu.VMEM((2 * TOPK, TOK), F32),
            dma((STEPS, 4)),
            dma((STEPS, 4)),
            dma((STEPS, 4)),
            dma((STEPS, 4)),
            dma((18,)),
            dma((18,)),
            dma((7,)),
            dma((7,)),
            dma((8,)),
        ],
        compiler_params=pltpu.CompilerParams(
            collective_id=0, has_side_effects=True, vmem_limit_bytes=66 * 1000 * 1000
        ),
        cost_estimate=pl.CostEstimate(
            flops=20_000_000_000, bytes_accessed=15_000_000, transcendentals=0
        ),
    )(
        w_down,
        out_grad[0],
        routes[0].T,
        gates[0].T,
        expert_slot.reshape(1, EXPERTS),
        saved,
    )
    hidden_grad = hidden_grad.reshape(LOCAL, CAP, NE, HID).transpose(0, 2, 1, 3)[None]
    return hidden_grad, gate_grad.T[None], weight_grad


def solution(mesh):
    return jax.shard_map(
        local,
        mesh=mesh,
        in_specs=(
            P("dp", "ep", None),
            P("dp", "ep", None),
            P("dp", "ep", None),
            P(),
            P("dp", "ep", None, None, None),
            P("dp", "ep"),
        ),
        out_specs=(P("dp", "ep", None, None, None), P("dp", "ep", None), P("dp", "ep")),
        check_vma=False,
    )
```

```python
import jax
import jax.numpy as jnp
from jax import lax
from jax.experimental import pallas as pl
from jax.experimental.pallas import tpu as pltpu
from jax.sharding import PartitionSpec as P

BF = jnp.bfloat16
F32 = jnp.float32
MESH = pl.DeviceIdType.MESH
NX, NY, NC, NZ = 4, 4, 2, 8
NE = NX * NY * NC
TOK, D, TOPK = 128, 2048, 8
EXPERTS, LOCAL, CAP, HID = 128, 4, 12, 768
DS = D // NZ
EXT = D + 2 * EXPERTS
ROWS = CAP * NE


def kernel(
    w_ref, og_ref, rt_ref, gt_ref, es_ref, hs_ref,
    hg_ref, gg_ref, wg_ref,
    T, W, X, Xf, G, S, Sf, H, Fst, Tm, Ub, Ur, SG, O, Pb, meta,
    ag_s, ag_r, rs_s, rs_r, tk_s, tk_r, sb_s, sb_r, sg_s, sg_r, ex_s, ex_r, loc, free,
):
    ep, z = lax.axis_index("ep"), lax.axis_index("dp")
    c, x, y = ep % NC, (ep // NC) % NX, ep // (NC * NX)

    def at(yy, xx, cc):
        return ((yy * NX + xx) * NC + cc, z)

    x_up, x_dn = (x + 1) % NX, (x + NX - 1) % NX
    y_up, y_dn = (y + 1) % NY, (y + NY - 1) % NY
    to_xu, to_xd, to_yu, to_yd = at(y, x_up, c), at(y, x_dn, c), at(y_up, x, c), at(y_dn, x, c)
    sibling = at(y, x, 1 - c)

    turn = (z + NZ + 1 - c) % NZ
    odd, pair = turn % 2, turn // 2
    sign = 2 * odd - 1
    role = [(pair + 1 - odd - sign * j + 8) % LOCAL for j in range(LOCAL)]

    def layer(offset):
        return (z + sign * offset + 2 * NZ) % NZ

    side = [(ep, layer(1)), (ep, layer(-1))]
    partner = side[1]
    way = [1 - odd, odd]

    barrier = pltpu.get_barrier_semaphore()
    for other in (side[0], side[1], to_xu, to_xd, to_yu, to_yd, sibling):
        pl.semaphore_signal(barrier, inc=1, device_id=other, device_id_type=MESH)
    pl.semaphore_wait(barrier, 7)

    def ag(flow, t, j):
        owner = layer(-t) if flow == 0 else layer(t)
        l = role[j]
        return pltpu.make_async_remote_copy(
            src_ref=w_ref.at[:, pl.ds(pl.multiple_of(l * HID, HID), HID)] if t == 0 else W.at[l, owner],
            dst_ref=W.at[l, owner],
            send_sem=ag_s.at[flow, j, t],
            recv_sem=ag_r.at[way[flow], l, t],
            device_id=side[flow],
            device_id_type=MESH,
        )

    def ag_list(t):
        fwd = [(0, t, j) for j in (0, 1, 2) if t <= 2 * j + 1]
        bwd = [(1, t, j) for j in (3, 2, 1) if t <= 6 - 2 * j]
        both = []
        for i in range(3):
            both += fwd[i : i + 1] + bwd[i : i + 1]
        return both

    def ag_step(t):
        for flow, t, j in ag_list(t):
            if t > 0:
                ag(flow, t - 1, j).wait_recv()
            ag(flow, t, j).start()

    ag_step(0)
    cx = (c, y, x // 2, x % 2)
    own_tokens = pltpu.make_async_copy(og_ref, T.at[(*cx, slice(None), pl.ds(0, D))], loc.at[0])
    own_tokens.start()
    own_saved = pltpu.make_async_copy(hs_ref, H, loc.at[1])
    own_saved.start()
    own_w = [
        pltpu.make_async_copy(w_ref.at[:, pl.ds(l * HID, HID)], W.at[l, z], loc.at[8 + l])
        for l in range(LOCAL)
    ]
    for copy in own_w:
        copy.start()

    io0 = lax.broadcasted_iota(jnp.int32, (EXPERTS, TOK), 0)
    io1 = lax.broadcasted_iota(jnp.int32, (EXPERTS, TOK), 1)
    es = es_ref[...]
    to_slot = (io0 == es).astype(F32).astype(BF)
    slot_of = jnp.transpose(jnp.broadcast_to(es.astype(F32), (EXPERTS, EXPERTS)))
    named = jnp.zeros((EXPERTS, TOK), F32)
    weight = jnp.zeros((EXPERTS, TOK), F32)
    for k in range(TOPK):
        hit = (io0 == rt_ref[k : k + 1, :]).astype(F32)
        named = named + hit
        weight = weight + hit * gt_ref[k : k + 1, :].astype(F32)
        meta[k : k + 1, :] = jnp.sum(hit * slot_of, axis=0, keepdims=True)
    earlier = (io0 < io1).astype(F32).astype(BF)
    rank = jnp.dot(named.astype(BF), earlier, preferred_element_type=F32)
    for k in range(TOPK):
        hit = (io0 == rt_ref[k : k + 1, :]).astype(F32)
        meta[TOPK + k : TOPK + k + 1, :] = jnp.sum(hit * rank, axis=0, keepdims=True)
    ranks = jnp.dot(to_slot, ((rank + 1.0) * named).astype(BF), preferred_element_type=F32)
    gates = jnp.dot(to_slot, weight.astype(BF), preferred_element_type=F32)
    T[c, y, x // 2, x % 2, :, D : D + EXPERTS] = ranks.astype(BF)
    T[c, y, x // 2, x % 2, :, D + EXPERTS : EXT] = jnp.transpose(gates).astype(BF)
    own_tokens.wait()

    half = TOK // 2
    up_rows, dn_rows = pl.ds(0, half), pl.ds(half, half)
    quarter = [pl.ds(i * half // 2, half // 2) for i in range(4)]
    every = slice(None)
    x_op, y_op = (x + 2) % NX, (y + 2) % NY

    def blocks(yy, xx, rows):
        if xx is every:
            return T.at[c, yy, :, :, rows]
        if yy is every:
            return T.at[c, :, xx // 2, xx % 2, rows]
        return T.at[c, yy, xx // 2, xx % 2, rows]

    def remote(ref, dst, send, recv, other):
        return pltpu.make_async_remote_copy(
            src_ref=ref, dst_ref=dst, send_sem=send, recv_sem=recv, device_id=other, device_id_type=MESH
        )

    def tk(n, ref, other):
        return remote(ref, ref, tk_s.at[n], tk_r.at[n], other)

    def sb(n, ref):
        return remote(ref, ref, sb_s.at[n], sb_r.at[n], sibling)

    tokens = [
        [
            tk(0, blocks(y, x, up_rows), to_xu),
            tk(1, blocks(y, x, up_rows), to_xd),
            tk(2, blocks(y, x, dn_rows), to_yu),
            tk(3, blocks(y, x, dn_rows), to_yd),
        ],
        [
            tk(4, blocks(y, x_dn, quarter[0]), to_xu),
            tk(5, blocks(y, x_up, quarter[1]), to_xd),
            tk(6, blocks(y_dn, x, quarter[2]), to_yu),
            tk(7, blocks(y_up, x, quarter[3]), to_yd),
        ],
        [
            tk(8, blocks(y, every, up_rows), to_yu),
            tk(9, blocks(y, every, up_rows), to_yd),
            tk(10, blocks(every, x, dn_rows), to_xu),
            tk(11, blocks(every, x, dn_rows), to_xd),
        ],
        [
            tk(12, blocks(y_dn, every, quarter[0]), to_yu),
            tk(13, blocks(y_up, every, quarter[1]), to_yd),
            tk(14, blocks(every, x_dn, quarter[2]), to_xu),
            tk(15, blocks(every, x_up, quarter[3]), to_xd),
        ],
        [],
    ]
    across = [
        [sb(0, blocks(y, x, pl.ds(0, TOK)))],
        [
            sb(1, blocks(y, x_dn, up_rows)),
            sb(2, blocks(y, x_up, up_rows)),
            sb(3, blocks(y_dn, x, dn_rows)),
            sb(4, blocks(y_up, x, dn_rows)),
        ],
        [sb(5, blocks(y, x_op, up_rows)), sb(6, blocks(y_op, x, dn_rows))],
        [
            sb(7, blocks(y_dn, every, up_rows)),
            sb(8, blocks(y_up, every, up_rows)),
            sb(9, blocks(every, x_dn, dn_rows)),
            sb(10, blocks(every, x_up, dn_rows)),
        ],
        [sb(11, blocks(y_op, every, up_rows)), sb(12, blocks(every, x_op, dn_rows))],
    ]

    def phase(n):
        if n > 0:
            for copy in tokens[n - 1]:
                copy.wait_recv()
        for copy in tokens[n] + across[n]:
            copy.start()

    phase(0)
    phase(1)
    phase(2)
    ag_step(1)
    phase(3)
    ag_step(2)
    phase(4)
    own_saved.wait()
    for copies in across:
        for copy in copies:
            copy.wait_recv()

    group = ROWS // 2
    io_row = lax.broadcasted_iota(jnp.int32, (group, TOK), 0).astype(F32)
    io16 = lax.broadcasted_iota(jnp.int32, (16, TOK), 0)
    first = pl.multiple_of((ep // 4) * 16, 16)
    wide = 256

    def pick_rows(l, a):
        for block in range(16):
            cc, yy, xx = block // 8, (block // 4) % 2, block % 4
            sixteen = T[cc, 2 * a + yy, xx // 2, xx % 2, pl.ds(first, 16), D : D + EXPERTS].astype(F32)
            v = jnp.sum(
                jnp.where(io16 == (ep % 4) * 4 + l, sixteen, 0.0), axis=0, keepdims=True
            )
            source = (yy * NX + xx) * NC + cc
            v = jnp.where(v > 0.5, 16.0 * v + (source - 16.0), -1.0)
            Pb[:, block * TOK : (block + 1) * TOK] = jnp.where(io_row == v, 1.0, 0.0).astype(BF)

        def pick(columns):
            both = [
                jnp.dot(
                    Pb[:, cc * 1024 : (cc + 1) * 1024],
                    T[cc, pl.ds(2 * a, 2), :, :, :, columns].reshape(1024, wide),
                    preferred_element_type=F32,
                )
                for cc in range(2)
            ]
            return both[0] + both[1]

        here = pl.ds(pl.multiple_of(a * 16, 16), 16)

        def tile(n, carry):
            columns = pl.ds(pl.multiple_of(n * wide, wide), wide)
            X[l, :, here, columns] = pick(columns).astype(BF).reshape(CAP, 16, wide)
            return carry

        lax.fori_loop(0, D // wide, tile, 0)
        last = pick(slice(D, EXT))
        lane = lax.broadcasted_iota(jnp.int32, (group, wide), 1)
        gate = jnp.sum(
            jnp.where(lane == EXPERTS + ep * LOCAL + l, last, 0.0), axis=1, keepdims=True
        )
        G[l, :, here, :] = jnp.broadcast_to(gate, (group, 128)).reshape(CAP, 16, 128)

    def build(j, carry):
        l = (pair + 1 - odd - sign * j + 8) % LOCAL

        def part(a, carry):
            pick_rows(l, a)
            return carry

        lax.fori_loop(0, 2, part, 0)
        gate = G[l].reshape(ROWS, 128)
        for n in range(HID // 128):
            columns = slice(n * 128, (n + 1) * 128)
            S[l, :, columns] = (gate * H[l, :, columns].astype(F32)).astype(BF)
        return carry

    give_rows = remote(X.at[role[3]], Xf, ex_s.at[0], ex_r.at[0], partner)
    give_scaled = remote(S.at[role[3]], Sf, ex_s.at[1], ex_r.at[1], partner)

    def build_and_serve(n, carry):
        build(3 - n, carry)

        @pl.when(n == 0)
        def _():
            give_scaled.start()
            give_rows.start()
            ag_step(3)

        @pl.when(n == 1)
        def _():
            ag_step(4)

        @pl.when(n == 2)
        def _():
            ag_step(5)

        return carry

    lax.fori_loop(0, LOCAL, build_and_serve, 0)

    for copies in tokens + across:
        for copy in copies:
            copy.wait_send()
    for other in side:
        pl.semaphore_signal(free, inc=1, device_id=other, device_id_type=MESH)

    def landing(l, slot):
        n = l * 9 + slot
        j = n // 3
        columns = pl.ds(pl.multiple_of((n % 3) * HID, HID), HID)
        return (j // 8, (j // 2) % 4, j % 2, slice(None), slice(None), columns)

    def term(j, offset, out, index):
        l, owner = role[j], layer(offset)
        there = pl.ds(pl.multiple_of(owner * DS, DS), DS)
        lhs = X[l, :, :, there].reshape(ROWS, DS)
        other = Xf[:, :, there].reshape(ROWS, DS) if j == 0 else None

        def tile(n, carry):
            columns = pl.ds(pl.multiple_of(n * wide, wide), wide)
            dims = (((0,), (0,)), ((), ()))
            both = lax.dot_general(lhs, S[l, :, columns], dims, preferred_element_type=F32)
            if j == 0:
                both = both + lax.dot_general(
                    other, Sf[:, columns], dims, preferred_element_type=F32
                )
            out[index, :, :, columns] = both.astype(BF).reshape(2, DS // 2, wide)
            return carry

        lax.fori_loop(0, HID // wide, tile, 0)

    def rs(flow, t, j, src):
        slot = 8 - t + 2 * j if flow == 0 else t - 5 + 2 * j
        return remote(
            src,
            T.at[landing(role[j], slot)],
            rs_s.at[flow, j, t],
            rs_r.at[way[flow], role[j], t],
            side[flow],
        )

    def arrived(flow, t, j):
        slot = t - (2 * j - 1) if flow == 0 else 12 - t - 2 * j
        ref = T.at[landing(role[j], slot)]
        remote(ref, ref, rs_s.at[flow, j, t], rs_r.at[way[flow], role[j], t], side[flow]).wait_recv()
        return landing(role[j], slot)

    def reach(flow, t):
        return 6 - t if flow == 0 else t - 6

    def rs_list(t):
        fwd = [(0, j) for j in (2, 1) if t >= 2 * j]
        bwd = [(1, j) for j in (0, 1, 2) if t >= 5 - 2 * j]
        return bwd + fwd if t < 2 else [v for p in zip(fwd + [None] * 3, bwd + [None] * 3) for v in p if v]

    sends = []

    def start(t):
        term(0, 6 - t, Fst, t)
        copy = rs(0, t, 0, Fst.at[t])
        copy.start()
        sends.append(copy)

    def rs_step(t):
        for flow, j in rs_list(t):
            here = arrived(flow, t - 1, j)
            T[here] = (T[here].astype(F32) + Tm[flow * 3 + j].astype(F32)).astype(BF)
            copy = rs(flow, t, j, T.at[here])
            copy.start()
            sends.append(copy)
        for flow, j in rs_list(t):
            if t < 5:
                term(j, reach(flow, t + 1), Tm, flow * 3 + j)

    term(2, reach(1, 1), Tm, 5)
    term(1, reach(0, 2), Tm, 1)
    term(1, reach(1, 3), Tm, 4)
    term(2, reach(0, 4), Tm, 2)
    pl.semaphore_wait(free, 2)
    give_scaled.wait_recv()
    give_rows.wait_recv()
    start(0)
    start(1)
    start(2)

    def u_tile(rows, l, n):
        columns = pl.ds(pl.multiple_of(n * wide, wide), wide)
        weights = W[l, :, :, columns].reshape(D, wide)
        return columns, jnp.dot(rows, weights, preferred_element_type=F32)

    def note(l, slot):
        lane = lax.broadcasted_iota(jnp.int32, (NE, 128), 1)
        mine = SG[c, y, x]
        for s in range(CAP):
            mine = jnp.where(lane == l * 16 + s, slot[s * NE : (s + 1) * NE, :], mine)
        SG[c, y, x] = mine

    def upstream(j, carry):
        l = (pair + 1 - odd - sign * j + 8) % LOCAL
        gate = jnp.concatenate([G[l].reshape(ROWS, 128)] * (wide // 128), axis=1)

        def tile(n, slot):
            columns, u = u_tile(X[l].reshape(ROWS, D), l, n)
            slot = slot + jnp.sum(H[l, :, columns].astype(F32) * u, axis=1, keepdims=True)
            H[l, :, columns] = (gate * u).astype(BF)
            return slot

        note(l, lax.fori_loop(0, HID // wide, tile, jnp.zeros((ROWS, 1), F32)))
        return carry

    def upstream_given():
        def tile(n, carry):
            columns, u = u_tile(Xf[...].reshape(ROWS, D), role[0], n)
            Ub[:, columns] = u.astype(BF)
            return carry

        lax.fori_loop(0, HID // wide, tile, 0)

    def upstream_away():
        l = role[3]
        gate = G[l].reshape(ROWS, 128)
        slot = jnp.zeros((ROWS, 1), F32)
        for n in range(HID // 128):
            columns = slice(n * 128, (n + 1) * 128)
            u = Ur[:, columns].astype(F32)
            slot = slot + jnp.sum(H[l, :, columns].astype(F32) * u, axis=1, keepdims=True)
            H[l, :, columns] = (gate * u).astype(BF)
        note(l, slot)

    out_hidden = pltpu.make_async_copy(H, hg_ref, loc.at[3])
    give_u = remote(Ub, Ur, ex_s.at[2], ex_r.at[2], partner)

    def sg(n, ref, other):
        return remote(ref, ref, sg_s.at[n], sg_r.at[n], other)

    slots = [
        [sg(0, SG.at[c, y, x], to_xu), sg(1, SG.at[c, y, x], to_xd)],
        [sg(2, SG.at[c, y, x_dn], to_xu)],
        [sg(3, SG.at[c, y], to_yu), sg(4, SG.at[c, y], to_yd)],
        [sg(5, SG.at[c, y_dn], to_yu)],
        [sg(6, SG.at[c], sibling)],
    ]

    def pass_on(n):
        if n > 0:
            for copy in slots[n - 1]:
                copy.wait_recv()
        for copy in slots[n]:
            copy.start()

    SG[c, y, x] = jnp.zeros((NE, 128), F32)

    rs_step(1)
    start(3)
    for t in range(6):
        ag(1, t, 0).wait_recv()
    for copy in own_w:
        copy.wait()
    upstream_given()
    give_u.start()
    rs_step(2)
    start(4)
    upstream(2, 0)
    rs_step(3)
    start(5)
    lax.fori_loop(0, 2, upstream, 0)
    rs_step(4)
    term(0, reach(1, 5), Tm, 3)
    give_u.wait_recv()
    upstream_away()
    out_hidden.start()
    pass_on(0)
    rs_step(5)
    pass_on(1)
    for j in range(3):
        term(j, 0, Tm, j)
    pass_on(2)
    pass_on(3)
    pass_on(4)
    slots[4][0].wait_recv()

    row = lax.broadcasted_iota(jnp.int32, (NE, NE, 128), 1)
    by_dev = jnp.sum(jnp.where(row == ep, SG[...].reshape(NE, NE, 128), 0.0), axis=1)
    high = by_dev.astype(BF)
    low = (by_dev - high.astype(F32)).astype(BF)
    io_dev = lax.broadcasted_iota(jnp.int32, (NE, TOK), 0)
    io_in = lax.broadcasted_iota(jnp.int32, (128, TOK), 0)
    for k in range(TOPK):
        q = meta[k : k + 1, :].astype(jnp.int32)
        r = meta[TOPK + k : TOPK + k + 1, :].astype(jnp.int32)
        device = lax.shift_right_logical(q, 2)
        place = lax.bitwise_and(device, 1) * 16 + lax.shift_right_logical(device, 1)
        pickers = (io_dev == place).astype(F32).astype(BF)
        found = sum(
            lax.dot_general(part, pickers, (((0,), (0,)), ((), ())), preferred_element_type=F32)
            for part in (high, low)
        )
        inside = lax.bitwise_and(q, 3) * 16 + r
        gg_ref[k : k + 1, :] = jnp.sum(
            jnp.where(io_in == inside, found, 0.0), axis=0, keepdims=True
        )

    outs = []
    for j, flows in ((3, (0,)), (2, (0, 1)), (1, (0, 1)), (0, (1,))):
        total = Tm[j].astype(F32) if j < 3 else None
        for flow in flows:
            part = T[arrived(flow, 5, j)].astype(F32)
            total = part if total is None else total + part
        l = role[j]
        O[l] = total.reshape(DS, HID)
        copy = pltpu.make_async_copy(
            O.at[l], wg_ref.at[:, pl.ds(pl.multiple_of(l * HID, HID), HID)], loc.at[4 + j]
        )
        copy.start()
        outs.append(copy)

    for t in range(6):
        for flow, t, j in ag_list(t):
            ag(flow, t, j).wait_send()
    for copy in sends + [give_scaled, give_rows, give_u]:
        copy.wait_send()
    for copies in slots:
        for copy in copies:
            copy.wait_send()
    out_hidden.wait()
    for copy in outs:
        copy.wait()


def local(out_grad, gates, routes, expert_slot, hidden_saved, w_down):
    hbm, vmem = pl.BlockSpec(memory_space=pl.ANY), pl.BlockSpec(memory_space=pltpu.VMEM)
    dma = pltpu.SemaphoreType.DMA
    saved = hidden_saved[0].transpose(0, 2, 1, 3).reshape(LOCAL, ROWS, HID)
    hidden_grad, gate_grad, weight_grad = pl.pallas_call(
        kernel,
        out_shape=(
            jax.ShapeDtypeStruct((LOCAL, ROWS, HID), BF),
            jax.ShapeDtypeStruct((TOPK, TOK), F32),
            jax.ShapeDtypeStruct((DS, LOCAL * HID), F32),
        ),
        in_specs=[hbm, hbm, vmem, vmem, vmem, hbm],
        out_specs=(hbm, vmem, hbm),
        scratch_shapes=[
            pltpu.VMEM((NC, NY, NX // 2, 2, TOK, EXT), BF),
            pltpu.VMEM((LOCAL, NZ, DS, HID), BF),
            pltpu.VMEM((LOCAL, CAP, NE, D), BF),
            pltpu.VMEM((CAP, NE, D), BF),
            pltpu.VMEM((LOCAL, CAP, NE, 128), F32),
            pltpu.VMEM((LOCAL, ROWS, HID), BF),
            pltpu.VMEM((ROWS, HID), BF),
            pltpu.VMEM((LOCAL, ROWS, HID), BF),
            pltpu.VMEM((6, 2, DS // 2, HID), BF),
            pltpu.VMEM((6, 2, DS // 2, HID), BF),
            pltpu.VMEM((ROWS, HID), BF),
            pltpu.VMEM((ROWS, HID), BF),
            pltpu.VMEM((NC, NY, NX, NE, 128), F32),
            pltpu.VMEM((LOCAL, DS, HID), F32),
            pltpu.VMEM((ROWS // 2, 16 * TOK), BF),
            pltpu.VMEM((2 * TOPK, TOK), F32),
            dma((2, LOCAL, 6)),
            dma((2, LOCAL, 6)),
            dma((2, LOCAL, 6)),
            dma((2, LOCAL, 6)),
            dma((16,)),
            dma((16,)),
            dma((13,)),
            dma((13,)),
            dma((7,)),
            dma((7,)),
            dma((3,)),
            dma((3,)),
            dma((12,)),
            pltpu.SemaphoreType.REGULAR,
        ],
        compiler_params=pltpu.CompilerParams(
            collective_id=0, has_side_effects=True, vmem_limit_bytes=66 * 1000 * 1000
        ),
        cost_estimate=pl.CostEstimate(
            flops=20_000_000_000, bytes_accessed=15_000_000, transcendentals=0
        ),
    )(
        w_down,
        out_grad[0],
        routes[0].T,
        gates[0].T,
        expert_slot.reshape(1, EXPERTS),
        saved,
    )
    hidden_grad = hidden_grad.reshape(LOCAL, CAP, NE, HID).transpose(0, 2, 1, 3)[None]
    return hidden_grad, gate_grad.T[None], weight_grad


def solution(mesh):
    return jax.shard_map(
        local,
        mesh=mesh,
        in_specs=(
            P("dp", "ep", None),
            P("dp", "ep", None),
            P("dp", "ep", None),
            P(),
            P("dp", "ep", None, None, None),
            P("dp", "ep"),
        ),
        out_specs=(P("dp", "ep", None, None, None), P("dp", "ep", None), P("dp", "ep")),
        check_vma=False,
    )
```

```python
import jax
import jax.numpy as jnp
from jax import lax
from jax.experimental import pallas as pl
from jax.experimental.pallas import tpu as pltpu
from jax.sharding import PartitionSpec as P

BF = jnp.bfloat16
F32 = jnp.float32
MESH = pl.DeviceIdType.MESH
NX, NY, NC, NZ = 4, 4, 2, 8
NE = NX * NY * NC
TOK, D, TOPK = 128, 2048, 8
EXPERTS, LOCAL, CAP, HID = 128, 4, 12, 768
DS = D // NZ
EXT = D + 2 * EXPERTS
ROWS = CAP * NE


def kernel(
    w_ref, og_ref, rt_ref, gt_ref, es_ref, hs_ref,
    H, gg_ref, O,
    T, W, X, Xf, G, S, Sf, Fst, Tm, Ub, Ur, SG, Pb, meta,
    ag_s, ag_r, rs_s, rs_r, tk_s, tk_r, sb_s, sb_r, sg_s, sg_r, ex_s, ex_r, loc, free,
):
    ep, z = lax.axis_index("ep"), lax.axis_index("dp")
    c, x, y = ep % NC, (ep // NC) % NX, ep // (NC * NX)

    def at(yy, xx, cc):
        return ((yy * NX + xx) * NC + cc, z)

    x_up, x_dn = (x + 1) % NX, (x + NX - 1) % NX
    y_up, y_dn = (y + 1) % NY, (y + NY - 1) % NY
    to_xu, to_xd, to_yu, to_yd = at(y, x_up, c), at(y, x_dn, c), at(y_up, x, c), at(y_dn, x, c)
    sibling = at(y, x, 1 - c)

    turn = (z + NZ + 1 - c) % NZ
    odd, pair = turn % 2, turn // 2
    sign = 2 * odd - 1
    role = [(pair + 1 - odd - sign * j + 8) % LOCAL for j in range(LOCAL)]

    def layer(offset):
        return (z + sign * offset + 2 * NZ) % NZ

    side = [(ep, layer(1)), (ep, layer(-1))]
    partner = side[1]
    way = [1 - odd, odd]

    barrier = pltpu.get_barrier_semaphore()
    for other in (side[0], side[1], to_xu, to_xd, to_yu, to_yd, sibling):
        pl.semaphore_signal(barrier, inc=1, device_id=other, device_id_type=MESH)
    pl.semaphore_wait(barrier, 7)

    def ag(flow, t, j):
        owner = layer(-t) if flow == 0 else layer(t)
        l = role[j]
        return pltpu.make_async_remote_copy(
            src_ref=w_ref.at[:, pl.ds(pl.multiple_of(l * HID, HID), HID)] if t == 0 else W.at[l, owner],
            dst_ref=W.at[l, owner],
            send_sem=ag_s.at[flow, j, t],
            recv_sem=ag_r.at[way[flow], l, t],
            device_id=side[flow],
            device_id_type=MESH,
        )

    def ag_list(t):
        fwd = [(0, t, j) for j in (0, 1, 2) if t <= 2 * j + 1]
        bwd = [(1, t, j) for j in (3, 2, 1) if t <= 6 - 2 * j]
        both = []
        for i in range(3):
            both += fwd[i : i + 1] + bwd[i : i + 1]
        return both

    def ag_step(t):
        for flow, t, j in ag_list(t):
            if t > 0:
                ag(flow, t - 1, j).wait_recv()
            ag(flow, t, j).start()

    ag_step(0)
    cx = (c, y, x // 2, x % 2)
    own_tokens = pltpu.make_async_copy(og_ref, T.at[(*cx, slice(None), pl.ds(0, D))], loc.at[0])
    own_tokens.start()
    own_saved = pltpu.make_async_copy(hs_ref, H, loc.at[1])
    own_saved.start()
    own_w = [
        pltpu.make_async_copy(w_ref.at[:, pl.ds(l * HID, HID)], W.at[l, z], loc.at[8 + l])
        for l in range(LOCAL)
    ]
    for copy in own_w:
        copy.start()

    io0 = lax.broadcasted_iota(jnp.int32, (EXPERTS, TOK), 0)
    io1 = lax.broadcasted_iota(jnp.int32, (EXPERTS, TOK), 1)
    es = es_ref[...]
    to_slot = (io0 == es).astype(F32).astype(BF)
    slot_of = jnp.transpose(jnp.broadcast_to(es.astype(F32), (EXPERTS, EXPERTS)))
    named = jnp.zeros((EXPERTS, TOK), F32)
    weight = jnp.zeros((EXPERTS, TOK), F32)
    for k in range(TOPK):
        hit = (io0 == rt_ref[k : k + 1, :]).astype(F32)
        named = named + hit
        weight = weight + hit * gt_ref[k : k + 1, :].astype(F32)
        meta[k : k + 1, :] = jnp.sum(hit * slot_of, axis=0, keepdims=True)
    earlier = (io0 < io1).astype(F32).astype(BF)
    rank = jnp.dot(named.astype(BF), earlier, preferred_element_type=F32)
    for k in range(TOPK):
        hit = (io0 == rt_ref[k : k + 1, :]).astype(F32)
        meta[TOPK + k : TOPK + k + 1, :] = jnp.sum(hit * rank, axis=0, keepdims=True)
    ranks = jnp.dot(to_slot, ((rank + 1.0) * named).astype(BF), preferred_element_type=F32)
    gates = jnp.dot(to_slot, weight.astype(BF), preferred_element_type=F32)
    T[c, y, x // 2, x % 2, :, D : D + EXPERTS] = ranks.astype(BF)
    T[c, y, x // 2, x % 2, :, D + EXPERTS : EXT] = jnp.transpose(gates).astype(BF)
    own_tokens.wait()

    half = TOK // 2
    up_rows, dn_rows = pl.ds(0, half), pl.ds(half, half)
    quarter = [pl.ds(i * half // 2, half // 2) for i in range(4)]
    every = slice(None)
    x_op, y_op = (x + 2) % NX, (y + 2) % NY

    def blocks(yy, xx, rows):
        if xx is every:
            return T.at[c, yy, :, :, rows]
        if yy is every:
            return T.at[c, :, xx // 2, xx % 2, rows]
        return T.at[c, yy, xx // 2, xx % 2, rows]

    def remote(ref, dst, send, recv, other):
        return pltpu.make_async_remote_copy(
            src_ref=ref, dst_ref=dst, send_sem=send, recv_sem=recv, device_id=other, device_id_type=MESH
        )

    def tk(n, ref, other):
        return remote(ref, ref, tk_s.at[n], tk_r.at[n], other)

    def sb(n, ref):
        return remote(ref, ref, sb_s.at[n], sb_r.at[n], sibling)

    tokens = [
        [
            tk(0, blocks(y, x, up_rows), to_xu),
            tk(1, blocks(y, x, up_rows), to_xd),
            tk(2, blocks(y, x, dn_rows), to_yu),
            tk(3, blocks(y, x, dn_rows), to_yd),
        ],
        [
            tk(4, blocks(y, x_dn, quarter[0]), to_xu),
            tk(5, blocks(y, x_up, quarter[1]), to_xd),
            tk(6, blocks(y_dn, x, quarter[2]), to_yu),
            tk(7, blocks(y_up, x, quarter[3]), to_yd),
        ],
        [
            tk(8, blocks(y, every, up_rows), to_yu),
            tk(9, blocks(y, every, up_rows), to_yd),
            tk(10, blocks(every, x, dn_rows), to_xu),
            tk(11, blocks(every, x, dn_rows), to_xd),
        ],
        [
            tk(12, blocks(y_dn, every, quarter[0]), to_yu),
            tk(13, blocks(y_up, every, quarter[1]), to_yd),
            tk(14, blocks(every, x_dn, quarter[2]), to_xu),
            tk(15, blocks(every, x_up, quarter[3]), to_xd),
        ],
        [],
    ]
    across = [
        [sb(0, blocks(y, x, pl.ds(0, TOK)))],
        [
            sb(1, blocks(y, x_dn, up_rows)),
            sb(2, blocks(y, x_up, up_rows)),
            sb(3, blocks(y_dn, x, dn_rows)),
            sb(4, blocks(y_up, x, dn_rows)),
        ],
        [sb(5, blocks(y, x_op, up_rows)), sb(6, blocks(y_op, x, dn_rows))],
        [
            sb(7, blocks(y_dn, every, up_rows)),
            sb(8, blocks(y_up, every, up_rows)),
            sb(9, blocks(every, x_dn, dn_rows)),
            sb(10, blocks(every, x_up, dn_rows)),
        ],
        [sb(11, blocks(y_op, every, up_rows)), sb(12, blocks(every, x_op, dn_rows))],
    ]

    def phase(n):
        if n > 0:
            for copy in tokens[n - 1]:
                copy.wait_recv()
        for copy in tokens[n] + across[n]:
            copy.start()

    phase(0)
    phase(1)
    phase(2)
    ag_step(1)
    phase(3)
    ag_step(2)
    phase(4)
    own_saved.wait()
    for copies in across:
        for copy in copies:
            copy.wait_recv()

    group = ROWS // 2
    io_row = lax.broadcasted_iota(jnp.int32, (group, TOK), 0).astype(F32)
    io16 = lax.broadcasted_iota(jnp.int32, (16, TOK), 0)
    first = pl.multiple_of((ep // 4) * 16, 16)
    wide = 256

    def pick_rows(ls, a):
        tall = len(ls) * group
        for block in range(16):
            cc, yy, xx = block // 8, (block // 4) % 2, block % 4
            sixteen = T[cc, 2 * a + yy, xx // 2, xx % 2, pl.ds(first, 16), D : D + EXPERTS].astype(F32)
            source = (yy * NX + xx) * NC + cc
            for i, l in enumerate(ls):
                v = jnp.sum(
                    jnp.where(io16 == (ep % 4) * 4 + l, sixteen, 0.0), axis=0, keepdims=True
                )
                v = jnp.where(v > 0.5, 16.0 * v + (source - 16.0), -1.0)
                Pb[i * group : (i + 1) * group, block * TOK : (block + 1) * TOK] = jnp.where(
                    io_row == v, 1.0, 0.0
                ).astype(BF)

        def pick(columns):
            both = [
                jnp.dot(
                    Pb[:tall, cc * 1024 : (cc + 1) * 1024],
                    T[cc, pl.ds(2 * a, 2), :, :, :, columns].reshape(1024, wide),
                    preferred_element_type=F32,
                )
                for cc in range(2)
            ]
            return both[0] + both[1]

        here = pl.ds(a * 16, 16)

        def tile(n, carry):
            columns = pl.ds(pl.multiple_of(n * wide, wide), wide)
            rows = pick(columns).astype(BF)
            for i, l in enumerate(ls):
                X[l, :, here, columns] = rows[i * group : (i + 1) * group].reshape(CAP, 16, wide)
            return carry

        lax.fori_loop(0, D // wide, tile, 0)
        last = pick(slice(D, EXT))
        lane = lax.broadcasted_iota(jnp.int32, (group, wide), 1)
        for i, l in enumerate(ls):
            gate = jnp.sum(
                jnp.where(
                    lane == EXPERTS + ep * LOCAL + l, last[i * group : (i + 1) * group], 0.0
                ),
                axis=1,
                keepdims=True,
            )
            G[l, :, here, :] = jnp.broadcast_to(gate, (group, 128)).reshape(CAP, 16, 128)

    def scale(l):
        gate = G[l].reshape(ROWS, 128)
        for n in range(HID // 128):
            columns = slice(n * 128, (n + 1) * 128)
            S[l, :, columns] = (gate * H[l, :, columns].astype(F32)).astype(BF)

    give_rows = remote(X.at[role[3]], Xf, ex_s.at[0], ex_r.at[0], partner)
    give_scaled = remote(S.at[role[3]], Sf, ex_s.at[1], ex_r.at[1], partner)

    pick_rows(role[3:], 0)
    pick_rows(role[3:], 1)
    give_rows.start()
    scale(role[3])
    give_scaled.start()
    ag_step(3)
    pick_rows(role[:3], 0)
    ag_step(4)
    pick_rows(role[:3], 1)
    ag_step(5)
    for l in role[:3]:
        scale(l)

    for copies in tokens + across:
        for copy in copies:
            copy.wait_send()
    for other in side:
        pl.semaphore_signal(free, inc=1, device_id=other, device_id_type=MESH)

    def landing(l, slot):
        n = l * 9 + slot
        j = n // 3
        columns = pl.ds(pl.multiple_of((n % 3) * HID, HID), HID)
        return (j // 8, (j // 2) % 4, j % 2, slice(None), slice(None), columns)

    def term(j, offset, out, index):
        l, owner = role[j], layer(offset)
        there = pl.ds(pl.multiple_of(owner * DS, DS), DS)
        lhs = X[l, :, :, there].reshape(ROWS, DS)
        other = Xf[:, :, there].reshape(ROWS, DS) if j == 0 else None

        def tile(n, carry):
            columns = pl.ds(pl.multiple_of(n * wide, wide), wide)
            dims = (((0,), (0,)), ((), ()))
            both = lax.dot_general(lhs, S[l, :, columns], dims, preferred_element_type=F32)
            if j == 0:
                both = both + lax.dot_general(
                    other, Sf[:, columns], dims, preferred_element_type=F32
                )
            out[index, :, :, columns] = both.astype(BF).reshape(2, DS // 2, wide)
            return carry

        lax.fori_loop(0, HID // wide, tile, 0)

    def rs(flow, t, j, src):
        slot = 8 - t + 2 * j if flow == 0 else t - 5 + 2 * j
        return remote(
            src,
            T.at[landing(role[j], slot)],
            rs_s.at[flow, j, t],
            rs_r.at[way[flow], role[j], t],
            side[flow],
        )

    def arrived(flow, t, j):
        slot = t - (2 * j - 1) if flow == 0 else 12 - t - 2 * j
        ref = T.at[landing(role[j], slot)]
        remote(ref, ref, rs_s.at[flow, j, t], rs_r.at[way[flow], role[j], t], side[flow]).wait_recv()
        return landing(role[j], slot)

    def reach(flow, t):
        return 6 - t if flow == 0 else t - 6

    def rs_list(t):
        fwd = [(0, j) for j in (2, 1) if t >= 2 * j]
        bwd = [(1, j) for j in (0, 1, 2) if t >= 5 - 2 * j]
        return bwd + fwd if t < 2 else [v for p in zip(fwd + [None] * 3, bwd + [None] * 3) for v in p if v]

    sends = []

    def start(t):
        term(0, 6 - t, Fst, t)
        copy = rs(0, t, 0, Fst.at[t])
        copy.start()
        sends.append(copy)

    def rs_step(t):
        for flow, j in rs_list(t):
            here = arrived(flow, t - 1, j)
            T[here] = (T[here].astype(F32) + Tm[flow * 3 + j].astype(F32)).astype(BF)
            copy = rs(flow, t, j, T.at[here])
            copy.start()
            sends.append(copy)
        for flow, j in rs_list(t):
            if t < 5:
                term(j, reach(flow, t + 1), Tm, flow * 3 + j)

    term(2, reach(1, 1), Tm, 5)
    term(1, reach(0, 2), Tm, 1)
    term(1, reach(1, 3), Tm, 4)
    term(2, reach(0, 4), Tm, 2)
    pl.semaphore_wait(free, 2)
    give_scaled.wait_recv()
    give_rows.wait_recv()
    start(0)
    start(1)
    start(2)

    def u_tile(rows, l, n):
        columns = pl.ds(pl.multiple_of(n * wide, wide), wide)
        weights = W[l, :, :, columns].reshape(D, wide)
        return columns, jnp.dot(rows, weights, preferred_element_type=F32)

    def note(l, slot):
        lane = lax.broadcasted_iota(jnp.int32, (NE, 128), 1)
        mine = SG[c, y, x]
        for s in range(CAP):
            mine = jnp.where(lane == l * 16 + s, slot[s * NE : (s + 1) * NE, :], mine)
        SG[c, y, x] = mine

    def upstream(j, carry):
        l = (pair + 1 - odd - sign * j + 8) % LOCAL
        gate = jnp.concatenate([G[l].reshape(ROWS, 128)] * (wide // 128), axis=1)

        def tile(n, slot):
            columns, u = u_tile(X[l].reshape(ROWS, D), l, n)
            slot = slot + jnp.sum(H[l, :, columns].astype(F32) * u, axis=1, keepdims=True)
            H[l, :, columns] = (gate * u).astype(BF)
            return slot

        note(l, lax.fori_loop(0, HID // wide, tile, jnp.zeros((ROWS, 1), F32)))
        return carry

    def upstream_given():
        def tile(n, carry):
            columns, u = u_tile(Xf[...].reshape(ROWS, D), role[0], n)
            Ub[:, columns] = u.astype(BF)
            return carry

        lax.fori_loop(0, HID // wide, tile, 0)

    def upstream_away():
        l = role[3]
        gate = G[l].reshape(ROWS, 128)
        slot = jnp.zeros((ROWS, 1), F32)
        for n in range(HID // 128):
            columns = slice(n * 128, (n + 1) * 128)
            u = Ur[:, columns].astype(F32)
            slot = slot + jnp.sum(H[l, :, columns].astype(F32) * u, axis=1, keepdims=True)
            H[l, :, columns] = (gate * u).astype(BF)
        note(l, slot)

    give_u = remote(Ub, Ur, ex_s.at[2], ex_r.at[2], partner)

    def sg(n, ref, other):
        return remote(ref, ref, sg_s.at[n], sg_r.at[n], other)

    slots = [
        [sg(0, SG.at[c, y, x], to_xu), sg(1, SG.at[c, y, x], to_xd)],
        [sg(2, SG.at[c, y, x_dn], to_xu)],
        [sg(3, SG.at[c, y], to_yu), sg(4, SG.at[c, y], to_yd)],
        [sg(5, SG.at[c, y_dn], to_yu)],
        [sg(6, SG.at[c], sibling)],
    ]

    def pass_on(n):
        if n > 0:
            for copy in slots[n - 1]:
                copy.wait_recv()
        for copy in slots[n]:
            copy.start()

    SG[c, y, x] = jnp.zeros((NE, 128), F32)

    rs_step(1)
    start(3)
    for t in range(6):
        ag(1, t, 0).wait_recv()
    for copy in own_w:
        copy.wait()
    upstream_given()
    give_u.start()
    rs_step(2)
    start(4)
    upstream(2, 0)
    rs_step(3)
    start(5)
    lax.fori_loop(0, 2, upstream, 0)
    rs_step(4)
    term(0, reach(1, 5), Tm, 3)
    give_u.wait_recv()
    upstream_away()
    pass_on(0)
    rs_step(5)
    pass_on(1)
    for j in range(3):
        term(j, 0, Tm, j)
    pass_on(2)
    pass_on(3)
    pass_on(4)
    slots[4][0].wait_recv()

    row = lax.broadcasted_iota(jnp.int32, (NE, NE, 128), 1)
    by_dev = jnp.sum(jnp.where(row == ep, SG[...].reshape(NE, NE, 128), 0.0), axis=1)
    high = by_dev.astype(BF)
    low = (by_dev - high.astype(F32)).astype(BF)
    io_dev = lax.broadcasted_iota(jnp.int32, (NE, TOK), 0)
    io_in = lax.broadcasted_iota(jnp.int32, (128, TOK), 0)
    for k in range(TOPK):
        q = meta[k : k + 1, :].astype(jnp.int32)
        r = meta[TOPK + k : TOPK + k + 1, :].astype(jnp.int32)
        device = lax.shift_right_logical(q, 2)
        place = lax.bitwise_and(device, 1) * 16 + lax.shift_right_logical(device, 1)
        pickers = (io_dev == place).astype(F32).astype(BF)
        found = sum(
            lax.dot_general(part, pickers, (((0,), (0,)), ((), ())), preferred_element_type=F32)
            for part in (high, low)
        )
        inside = lax.bitwise_and(q, 3) * 16 + r
        gg_ref[k : k + 1, :] = jnp.sum(
            jnp.where(io_in == inside, found, 0.0), axis=0, keepdims=True
        )

    for j, flows in ((3, (0,)), (2, (0, 1)), (1, (0, 1)), (0, (1,))):
        total = Tm[j].astype(F32) if j < 3 else None
        for flow in flows:
            part = T[arrived(flow, 5, j)].astype(F32)
            total = part if total is None else total + part
        l = role[j]
        O[:, pl.ds(pl.multiple_of(l * HID, HID), HID)] = total.reshape(DS, HID)

    for t in range(6):
        for flow, t, j in ag_list(t):
            ag(flow, t, j).wait_send()
    for copy in sends + [give_scaled, give_rows, give_u]:
        copy.wait_send()
    for copies in slots:
        for copy in copies:
            copy.wait_send()


def local(out_grad, gates, routes, expert_slot, hidden_saved, w_down):
    hbm, vmem = pl.BlockSpec(memory_space=pl.ANY), pl.BlockSpec(memory_space=pltpu.VMEM)
    dma = pltpu.SemaphoreType.DMA
    saved = hidden_saved[0].transpose(0, 2, 1, 3).reshape(LOCAL, ROWS, HID)
    hidden_grad, gate_grad, weight_grad = pl.pallas_call(
        kernel,
        out_shape=(
            pltpu.VMEM((LOCAL, ROWS, HID), BF),
            pltpu.VMEM((TOPK, TOK), F32),
            pltpu.VMEM((DS, LOCAL * HID), F32),
        ),
        in_specs=[hbm, hbm, vmem, vmem, vmem, hbm],
        out_specs=(vmem, vmem, vmem),
        scratch_shapes=[
            pltpu.VMEM((NC, NY, NX // 2, 2, TOK, EXT), BF),
            pltpu.VMEM((LOCAL, NZ, DS, HID), BF),
            pltpu.VMEM((LOCAL, CAP, NE, D), BF),
            pltpu.VMEM((CAP, NE, D), BF),
            pltpu.VMEM((LOCAL, CAP, NE, 128), F32),
            pltpu.VMEM((LOCAL, ROWS, HID), BF),
            pltpu.VMEM((ROWS, HID), BF),
            pltpu.VMEM((6, 2, DS // 2, HID), BF),
            pltpu.VMEM((6, 2, DS // 2, HID), BF),
            pltpu.VMEM((ROWS, HID), BF),
            pltpu.VMEM((ROWS, HID), BF),
            pltpu.VMEM((NC, NY, NX, NE, 128), F32),
            pltpu.VMEM((3 * ROWS // 2, 16 * TOK), BF),
            pltpu.VMEM((2 * TOPK, TOK), F32),
            dma((2, LOCAL, 6)),
            dma((2, LOCAL, 6)),
            dma((2, LOCAL, 6)),
            dma((2, LOCAL, 6)),
            dma((16,)),
            dma((16,)),
            dma((13,)),
            dma((13,)),
            dma((7,)),
            dma((7,)),
            dma((3,)),
            dma((3,)),
            dma((12,)),
            pltpu.SemaphoreType.REGULAR,
        ],
        compiler_params=pltpu.CompilerParams(
            collective_id=0, has_side_effects=True, vmem_limit_bytes=57 * 1000 * 1000
        ),
        cost_estimate=pl.CostEstimate(
            flops=20_000_000_000, bytes_accessed=15_000_000, transcendentals=0
        ),
    )(
        w_down,
        out_grad[0],
        routes[0].T,
        gates[0].T,
        expert_slot.reshape(1, EXPERTS),
        saved,
    )
    hidden_grad = hidden_grad.reshape(LOCAL, CAP, NE, HID).transpose(0, 2, 1, 3)[None]
    return hidden_grad, gate_grad.T[None], weight_grad


def solution(mesh):
    return jax.shard_map(
        local,
        mesh=mesh,
        in_specs=(
            P("dp", "ep", None),
            P("dp", "ep", None),
            P("dp", "ep", None),
            P(),
            P("dp", "ep", None, None, None),
            P("dp", "ep"),
        ),
        out_specs=(P("dp", "ep", None, None, None), P("dp", "ep", None), P("dp", "ep")),
        check_vma=False,
    )
```

```python
import jax
import jax.numpy as jnp
from jax import lax
from jax.experimental import pallas as pl
from jax.experimental.pallas import tpu as pltpu
from jax.sharding import PartitionSpec as P

BF = jnp.bfloat16
F32 = jnp.float32
MESH = pl.DeviceIdType.MESH
NX, NY, NC, NZ = 4, 4, 2, 8
NE = NX * NY * NC
TOK, D, TOPK = 128, 2048, 8
EXPERTS, LOCAL, CAP, HID = 128, 4, 12, 768
DS = D // NZ
EXT = D + 2 * EXPERTS
ROWS = CAP * NE


def kernel(
    w_ref, og_ref, rt_ref, gt_ref, es_ref, hs_ref,
    H, gg_ref, O,
    T, W, X, Xf, G, S, Sf, Fst, Tm, Ub, Ur, SG, Pb, meta,
    ag_s, ag_r, rs_s, rs_r, tk_s, tk_r, sb_s, sb_r, sg_s, sg_r, ex_s, ex_r, loc, free,
):
    ep, z = lax.axis_index("ep"), lax.axis_index("dp")
    c, x, y = ep % NC, (ep // NC) % NX, ep // (NC * NX)

    def at(yy, xx, cc):
        return ((yy * NX + xx) * NC + cc, z)

    x_up, x_dn = (x + 1) % NX, (x + NX - 1) % NX
    y_up, y_dn = (y + 1) % NY, (y + NY - 1) % NY
    to_xu, to_xd, to_yu, to_yd = at(y, x_up, c), at(y, x_dn, c), at(y_up, x, c), at(y_dn, x, c)
    sibling = at(y, x, 1 - c)

    turn = (z + NZ + 1 - c) % NZ
    odd, pair = turn % 2, turn // 2
    sign = 2 * odd - 1
    role = [(pair + 1 - odd - sign * j + 8) % LOCAL for j in range(LOCAL)]

    def layer(offset):
        return (z + sign * offset + 2 * NZ) % NZ

    side = [(ep, layer(1)), (ep, layer(-1))]
    partner = side[1]
    way = [1 - odd, odd]

    barrier = pltpu.get_barrier_semaphore()
    for other in (side[0], side[1], to_xu, to_xd, to_yu, to_yd, sibling):
        pl.semaphore_signal(barrier, inc=1, device_id=other, device_id_type=MESH)
    pl.semaphore_wait(barrier, 7)

    def ag(flow, t, j):
        owner = layer(-t) if flow == 0 else layer(t)
        l = role[j]
        return pltpu.make_async_remote_copy(
            src_ref=w_ref.at[:, pl.ds(pl.multiple_of(l * HID, HID), HID)] if t == 0 else W.at[l, owner],
            dst_ref=W.at[l, owner],
            send_sem=ag_s.at[flow, j, t],
            recv_sem=ag_r.at[way[flow], l, t],
            device_id=side[flow],
            device_id_type=MESH,
        )

    def ag_list(t):
        fwd = [(0, t, j) for j in (0, 1, 2) if t <= 2 * j + 1]
        bwd = [(1, t, j) for j in (3, 2, 1) if t <= 6 - 2 * j]
        both = []
        for i in range(3):
            both += fwd[i : i + 1] + bwd[i : i + 1]
        return both

    def ag_step(t):
        for flow, t, j in ag_list(t):
            if t > 0:
                ag(flow, t - 1, j).wait_recv()
            ag(flow, t, j).start()

    ag_step(0)
    cx = (c, y, x // 2, x % 2)
    own_tokens = pltpu.make_async_copy(og_ref, T.at[(*cx, slice(None), pl.ds(0, D))], loc.at[0])
    own_tokens.start()
    own_saved = pltpu.make_async_copy(hs_ref, H, loc.at[1])
    own_saved.start()
    own_w = [
        pltpu.make_async_copy(w_ref.at[:, pl.ds(l * HID, HID)], W.at[l, z], loc.at[8 + l])
        for l in range(LOCAL)
    ]
    for copy in own_w:
        copy.start()

    io0 = lax.broadcasted_iota(jnp.int32, (EXPERTS, TOK), 0)
    io1 = lax.broadcasted_iota(jnp.int32, (EXPERTS, TOK), 1)
    es = es_ref[...]
    to_slot = (io0 == es).astype(F32).astype(BF)
    slot_of = jnp.transpose(jnp.broadcast_to(es.astype(F32), (EXPERTS, EXPERTS)))
    named = jnp.zeros((EXPERTS, TOK), F32)
    weight = jnp.zeros((EXPERTS, TOK), F32)
    for k in range(TOPK):
        hit = (io0 == rt_ref[k : k + 1, :]).astype(F32)
        named = named + hit
        weight = weight + hit * gt_ref[k : k + 1, :].astype(F32)
        meta[k : k + 1, :] = jnp.sum(hit * slot_of, axis=0, keepdims=True)
    earlier = (io0 < io1).astype(F32).astype(BF)
    rank = jnp.dot(named.astype(BF), earlier, preferred_element_type=F32)
    for k in range(TOPK):
        hit = (io0 == rt_ref[k : k + 1, :]).astype(F32)
        meta[TOPK + k : TOPK + k + 1, :] = jnp.sum(hit * rank, axis=0, keepdims=True)
    ranks = jnp.dot(to_slot, ((rank + 1.0) * named).astype(BF), preferred_element_type=F32)
    gates = jnp.dot(to_slot, weight.astype(BF), preferred_element_type=F32)
    T[c, y, x // 2, x % 2, :, D : D + EXPERTS] = ranks.astype(BF)
    T[c, y, x // 2, x % 2, :, D + EXPERTS : EXT] = jnp.transpose(gates).astype(BF)
    own_tokens.wait()

    half = TOK // 2
    up_rows, dn_rows = pl.ds(0, half), pl.ds(half, half)
    quarter = [pl.ds(i * half // 2, half // 2) for i in range(4)]
    every = slice(None)
    x_op, y_op = (x + 2) % NX, (y + 2) % NY

    def blocks(yy, xx, rows):
        if xx is every:
            return T.at[c, yy, :, :, rows]
        if yy is every:
            return T.at[c, :, xx // 2, xx % 2, rows]
        return T.at[c, yy, xx // 2, xx % 2, rows]

    def remote(ref, dst, send, recv, other):
        return pltpu.make_async_remote_copy(
            src_ref=ref, dst_ref=dst, send_sem=send, recv_sem=recv, device_id=other, device_id_type=MESH
        )

    def tk(n, ref, other):
        return remote(ref, ref, tk_s.at[n], tk_r.at[n], other)

    def sb(n, ref):
        return remote(ref, ref, sb_s.at[n], sb_r.at[n], sibling)

    tokens = [
        [
            tk(0, blocks(y, x, up_rows), to_xu),
            tk(1, blocks(y, x, up_rows), to_xd),
            tk(2, blocks(y, x, dn_rows), to_yu),
            tk(3, blocks(y, x, dn_rows), to_yd),
        ],
        [
            tk(4, blocks(y, x_dn, quarter[0]), to_xu),
            tk(5, blocks(y, x_up, quarter[1]), to_xd),
            tk(6, blocks(y_dn, x, quarter[2]), to_yu),
            tk(7, blocks(y_up, x, quarter[3]), to_yd),
        ],
        [
            tk(8, blocks(y, every, up_rows), to_yu),
            tk(9, blocks(y, every, up_rows), to_yd),
            tk(10, blocks(every, x, dn_rows), to_xu),
            tk(11, blocks(every, x, dn_rows), to_xd),
        ],
        [
            tk(12, blocks(y_dn, every, quarter[0]), to_yu),
            tk(13, blocks(y_up, every, quarter[1]), to_yd),
            tk(14, blocks(every, x_dn, quarter[2]), to_xu),
            tk(15, blocks(every, x_up, quarter[3]), to_xd),
        ],
        [],
    ]
    across = [
        [sb(0, blocks(y, x, pl.ds(0, TOK)))],
        [
            sb(1, blocks(y, x_dn, up_rows)),
            sb(2, blocks(y, x_up, up_rows)),
            sb(3, blocks(y_dn, x, dn_rows)),
            sb(4, blocks(y_up, x, dn_rows)),
        ],
        [sb(5, blocks(y, x_op, up_rows)), sb(6, blocks(y_op, x, dn_rows))],
        [
            sb(7, blocks(y_dn, every, up_rows)),
            sb(8, blocks(y_up, every, up_rows)),
            sb(9, blocks(every, x_dn, dn_rows)),
            sb(10, blocks(every, x_up, dn_rows)),
        ],
        [sb(11, blocks(y_op, every, up_rows)), sb(12, blocks(every, x_op, dn_rows))],
    ]

    def phase(n):
        if n > 0:
            for copy in tokens[n - 1]:
                copy.wait_recv()
        for copy in tokens[n] + across[n]:
            copy.start()

    phase(0)
    phase(1)
    phase(2)
    ag_step(1)
    phase(3)
    ag_step(2)
    phase(4)
    own_saved.wait()
    for copies in across:
        for copy in copies:
            copy.wait_recv()

    group = ROWS // 2
    io_row = lax.broadcasted_iota(jnp.int32, (group, TOK), 0).astype(F32)
    io16 = lax.broadcasted_iota(jnp.int32, (16, TOK), 0)
    first = pl.multiple_of((ep // 4) * 16, 16)
    wide = 256

    def pick_rows(ls, a):
        tall = len(ls) * group
        for block in range(16):
            cc, yy, xx = block // 8, (block // 4) % 2, block % 4
            sixteen = T[cc, 2 * a + yy, xx // 2, xx % 2, pl.ds(first, 16), D : D + EXPERTS].astype(F32)
            source = (yy * NX + xx) * NC + cc
            for i, l in enumerate(ls):
                v = jnp.sum(
                    jnp.where(io16 == (ep % 4) * 4 + l, sixteen, 0.0), axis=0, keepdims=True
                )
                v = jnp.where(v > 0.5, 16.0 * v + (source - 16.0), -1.0)
                Pb[i * group : (i + 1) * group, block * TOK : (block + 1) * TOK] = jnp.where(
                    io_row == v, 1.0, 0.0
                ).astype(BF)

        def pick(columns):
            both = [
                jnp.dot(
                    Pb[:tall, cc * 1024 : (cc + 1) * 1024],
                    T[cc, pl.ds(2 * a, 2), :, :, :, columns].reshape(1024, wide),
                    preferred_element_type=F32,
                )
                for cc in range(2)
            ]
            return both[0] + both[1]

        here = pl.ds(a * 16, 16)

        def tile(n, carry):
            columns = pl.ds(pl.multiple_of(n * wide, wide), wide)
            rows = pick(columns).astype(BF)
            for i, l in enumerate(ls):
                X[l, :, here, columns] = rows[i * group : (i + 1) * group].reshape(CAP, 16, wide)
            return carry

        lax.fori_loop(0, D // wide, tile, 0)
        last = pick(slice(D, EXT))
        lane = lax.broadcasted_iota(jnp.int32, (group, wide), 1)
        for i, l in enumerate(ls):
            gate = jnp.sum(
                jnp.where(
                    lane == EXPERTS + ep * LOCAL + l, last[i * group : (i + 1) * group], 0.0
                ),
                axis=1,
                keepdims=True,
            )
            G[l, :, here, :] = jnp.broadcast_to(gate, (group, 128)).reshape(CAP, 16, 128)

    def scale(l):
        gate = G[l].reshape(ROWS, 128)
        for n in range(HID // 128):
            columns = slice(n * 128, (n + 1) * 128)
            S[l, :, columns] = (gate * H[l, :, columns].astype(F32)).astype(BF)

    give_rows = remote(X.at[role[3]], Xf, ex_s.at[0], ex_r.at[0], partner)
    give_scaled = remote(S.at[role[3]], Sf, ex_s.at[1], ex_r.at[1], partner)

    pick_rows(role[3:], 0)
    pick_rows(role[3:], 1)
    give_rows.start()
    scale(role[3])
    give_scaled.start()
    ag_step(3)
    pick_rows(role[:3], 0)
    pick_rows(role[:3], 1)
    for l in role[:3]:
        scale(l)

    for copies in tokens + across:
        for copy in copies:
            copy.wait_send()
    for other in side:
        pl.semaphore_signal(free, inc=1, device_id=other, device_id_type=MESH)

    def landing(l, slot):
        n = l * 9 + slot
        j = n // 3
        columns = pl.ds(pl.multiple_of((n % 3) * HID, HID), HID)
        return (j // 8, (j // 2) % 4, j % 2, slice(None), slice(None), columns)

    def term(j, offset, out, index):
        l, owner = role[j], layer(offset)
        there = pl.ds(pl.multiple_of(owner * DS, DS), DS)
        lhs = X[l, :, :, there].reshape(ROWS, DS)
        other = Xf[:, :, there].reshape(ROWS, DS) if j == 0 else None

        def tile(n, carry):
            columns = pl.ds(pl.multiple_of(n * wide, wide), wide)
            dims = (((0,), (0,)), ((), ()))
            both = lax.dot_general(lhs, S[l, :, columns], dims, preferred_element_type=F32)
            if j == 0:
                both = both + lax.dot_general(
                    other, Sf[:, columns], dims, preferred_element_type=F32
                )
            out[index, :, :, columns] = both.astype(BF).reshape(2, DS // 2, wide)
            return carry

        lax.fori_loop(0, HID // wide, tile, 0)

    def rs(flow, t, j, src):
        slot = 8 - t + 2 * j if flow == 0 else t - 5 + 2 * j
        return remote(
            src,
            T.at[landing(role[j], slot)],
            rs_s.at[flow, j, t],
            rs_r.at[way[flow], role[j], t],
            side[flow],
        )

    def arrived(flow, t, j):
        slot = t - (2 * j - 1) if flow == 0 else 12 - t - 2 * j
        ref = T.at[landing(role[j], slot)]
        remote(ref, ref, rs_s.at[flow, j, t], rs_r.at[way[flow], role[j], t], side[flow]).wait_recv()
        return landing(role[j], slot)

    def reach(flow, t):
        return 6 - t if flow == 0 else t - 6

    def rs_list(t):
        fwd = [(0, j) for j in (2, 1) if t >= 2 * j]
        bwd = [(1, j) for j in (0, 1, 2) if t >= 5 - 2 * j]
        return bwd + fwd if t < 2 else [v for p in zip(fwd + [None] * 3, bwd + [None] * 3) for v in p if v]

    sends = []

    def start(t):
        term(0, 6 - t, Fst, t)
        copy = rs(0, t, 0, Fst.at[t])
        copy.start()
        sends.append(copy)

    def rs_step(t):
        for flow, j in rs_list(t):
            here = arrived(flow, t - 1, j)
            T[here] = (T[here].astype(F32) + Tm[flow * 3 + j].astype(F32)).astype(BF)
            copy = rs(flow, t, j, T.at[here])
            copy.start()
            sends.append(copy)
        for flow, j in rs_list(t):
            if t < 5:
                term(j, reach(flow, t + 1), Tm, flow * 3 + j)

    term(2, reach(1, 1), Tm, 5)
    term(1, reach(0, 2), Tm, 1)
    term(1, reach(1, 3), Tm, 4)
    term(2, reach(0, 4), Tm, 2)
    pl.semaphore_wait(free, 2)
    give_scaled.wait_recv()
    give_rows.wait_recv()
    start(0)
    start(1)
    ag_step(4)
    start(2)

    def u_tile(rows, l, n):
        columns = pl.ds(pl.multiple_of(n * wide, wide), wide)
        weights = W[l, :, :, columns].reshape(D, wide)
        return columns, jnp.dot(rows, weights, preferred_element_type=F32)

    def note(l, slot):
        lane = lax.broadcasted_iota(jnp.int32, (NE, 128), 1)
        mine = SG[c, y, x]
        for s in range(CAP):
            mine = jnp.where(lane == l * 16 + s, slot[s * NE : (s + 1) * NE, :], mine)
        SG[c, y, x] = mine

    def upstream(j, carry):
        l = (pair + 1 - odd - sign * j + 8) % LOCAL
        gate = jnp.concatenate([G[l].reshape(ROWS, 128)] * (wide // 128), axis=1)

        def tile(n, slot):
            columns, u = u_tile(X[l].reshape(ROWS, D), l, n)
            slot = slot + jnp.sum(H[l, :, columns].astype(F32) * u, axis=1, keepdims=True)
            H[l, :, columns] = (gate * u).astype(BF)
            return slot

        note(l, lax.fori_loop(0, HID // wide, tile, jnp.zeros((ROWS, 1), F32)))
        return carry

    def upstream_given():
        def tile(n, carry):
            columns, u = u_tile(Xf[...].reshape(ROWS, D), role[0], n)
            Ub[:, columns] = u.astype(BF)
            return carry

        lax.fori_loop(0, HID // wide, tile, 0)

    def upstream_away():
        l = role[3]
        gate = G[l].reshape(ROWS, 128)
        slot = jnp.zeros((ROWS, 1), F32)
        for n in range(HID // 128):
            columns = slice(n * 128, (n + 1) * 128)
            u = Ur[:, columns].astype(F32)
            slot = slot + jnp.sum(H[l, :, columns].astype(F32) * u, axis=1, keepdims=True)
            H[l, :, columns] = (gate * u).astype(BF)
        note(l, slot)

    give_u = remote(Ub, Ur, ex_s.at[2], ex_r.at[2], partner)

    def sg(n, ref, other):
        return remote(ref, ref, sg_s.at[n], sg_r.at[n], other)

    slots = [
        [sg(0, SG.at[c, y, x], to_xu), sg(1, SG.at[c, y, x], to_xd)],
        [sg(2, SG.at[c, y, x_dn], to_xu)],
        [sg(3, SG.at[c, y], to_yu), sg(4, SG.at[c, y], to_yd)],
        [sg(5, SG.at[c, y_dn], to_yu)],
        [sg(6, SG.at[c], sibling)],
    ]

    def pass_on(n):
        if n > 0:
            for copy in slots[n - 1]:
                copy.wait_recv()
        for copy in slots[n]:
            copy.start()

    SG[c, y, x] = jnp.zeros((NE, 128), F32)

    rs_step(1)
    start(3)
    ag_step(5)
    rs_step(2)
    start(4)
    for t in range(6):
        ag(1, t, 0).wait_recv()
    for copy in own_w:
        copy.wait()
    upstream_given()
    give_u.start()
    rs_step(3)
    start(5)
    upstream(2, 0)
    rs_step(4)
    lax.fori_loop(0, 2, upstream, 0)
    term(0, reach(1, 5), Tm, 3)
    give_u.wait_recv()
    upstream_away()
    pass_on(0)
    rs_step(5)
    pass_on(1)
    for j in range(3):
        term(j, 0, Tm, j)
    pass_on(2)
    pass_on(3)
    pass_on(4)
    slots[4][0].wait_recv()

    row = lax.broadcasted_iota(jnp.int32, (NE, NE, 128), 1)
    by_dev = jnp.sum(jnp.where(row == ep, SG[...].reshape(NE, NE, 128), 0.0), axis=1)
    high = by_dev.astype(BF)
    low = (by_dev - high.astype(F32)).astype(BF)
    io_dev = lax.broadcasted_iota(jnp.int32, (NE, TOK), 0)
    io_in = lax.broadcasted_iota(jnp.int32, (128, TOK), 0)
    for k in range(TOPK):
        q = meta[k : k + 1, :].astype(jnp.int32)
        r = meta[TOPK + k : TOPK + k + 1, :].astype(jnp.int32)
        device = lax.shift_right_logical(q, 2)
        place = lax.bitwise_and(device, 1) * 16 + lax.shift_right_logical(device, 1)
        pickers = (io_dev == place).astype(F32).astype(BF)
        found = sum(
            lax.dot_general(part, pickers, (((0,), (0,)), ((), ())), preferred_element_type=F32)
            for part in (high, low)
        )
        inside = lax.bitwise_and(q, 3) * 16 + r
        gg_ref[k : k + 1, :] = jnp.sum(
            jnp.where(io_in == inside, found, 0.0), axis=0, keepdims=True
        )

    for j, flows in ((3, (0,)), (2, (0, 1)), (1, (0, 1)), (0, (1,))):
        total = Tm[j].astype(F32) if j < 3 else None
        for flow in flows:
            part = T[arrived(flow, 5, j)].astype(F32)
            total = part if total is None else total + part
        l = role[j]
        O[:, pl.ds(pl.multiple_of(l * HID, HID), HID)] = total.reshape(DS, HID)

    for t in range(6):
        for flow, t, j in ag_list(t):
            ag(flow, t, j).wait_send()
    for copy in sends + [give_scaled, give_rows, give_u]:
        copy.wait_send()
    for copies in slots:
        for copy in copies:
            copy.wait_send()


def write(h_ref, g_ref, w_ref, h_out, g_out, w_out, sem):
    pairs = ((w_ref, w_out), (h_ref, h_out), (g_ref, g_out))
    copies = [pltpu.make_async_copy(a, b, sem.at[i]) for i, (a, b) in enumerate(pairs)]
    for copy in copies:
        copy.start()
    for copy in copies:
        copy.wait()


def local(out_grad, gates, routes, expert_slot, hidden_saved, w_down):
    hbm, vmem = pl.BlockSpec(memory_space=pl.ANY), pl.BlockSpec(memory_space=pltpu.VMEM)
    dma = pltpu.SemaphoreType.DMA
    saved = hidden_saved[0].transpose(0, 2, 1, 3).reshape(LOCAL, ROWS, HID)
    hidden_grad, gate_grad, weight_grad = pl.pallas_call(
        kernel,
        out_shape=(
            pltpu.VMEM((LOCAL, ROWS, HID), BF),
            pltpu.VMEM((TOPK, TOK), F32),
            pltpu.VMEM((DS, LOCAL * HID), F32),
        ),
        in_specs=[hbm, hbm, vmem, vmem, vmem, hbm],
        out_specs=(vmem, vmem, vmem),
        scratch_shapes=[
            pltpu.VMEM((NC, NY, NX // 2, 2, TOK, EXT), BF),
            pltpu.VMEM((LOCAL, NZ, DS, HID), BF),
            pltpu.VMEM((LOCAL, CAP, NE, D), BF),
            pltpu.VMEM((CAP, NE, D), BF),
            pltpu.VMEM((LOCAL, CAP, NE, 128), F32),
            pltpu.VMEM((LOCAL, ROWS, HID), BF),
            pltpu.VMEM((ROWS, HID), BF),
            pltpu.VMEM((6, 2, DS // 2, HID), BF),
            pltpu.VMEM((6, 2, DS // 2, HID), BF),
            pltpu.VMEM((ROWS, HID), BF),
            pltpu.VMEM((ROWS, HID), BF),
            pltpu.VMEM((NC, NY, NX, NE, 128), F32),
            pltpu.VMEM((3 * ROWS // 2, 16 * TOK), BF),
            pltpu.VMEM((2 * TOPK, TOK), F32),
            dma((2, LOCAL, 6)),
            dma((2, LOCAL, 6)),
            dma((2, LOCAL, 6)),
            dma((2, LOCAL, 6)),
            dma((16,)),
            dma((16,)),
            dma((13,)),
            dma((13,)),
            dma((7,)),
            dma((7,)),
            dma((3,)),
            dma((3,)),
            dma((12,)),
            pltpu.SemaphoreType.REGULAR,
        ],
        compiler_params=pltpu.CompilerParams(
            collective_id=0, has_side_effects=True, vmem_limit_bytes=57 * 1000 * 1000
        ),
        cost_estimate=pl.CostEstimate(
            flops=20_000_000_000, bytes_accessed=15_000_000, transcendentals=0
        ),
    )(
        w_down,
        out_grad[0],
        routes[0].T,
        gates[0].T,
        expert_slot.reshape(1, EXPERTS),
        saved,
    )
    hidden_grad, gate_grad, weight_grad = pl.pallas_call(
        write,
        out_shape=(
            jax.ShapeDtypeStruct((LOCAL, ROWS, HID), BF),
            jax.ShapeDtypeStruct((TOPK, TOK), F32),
            jax.ShapeDtypeStruct((DS, LOCAL * HID), F32),
        ),
        in_specs=[vmem, vmem, vmem],
        out_specs=(hbm, hbm, hbm),
        scratch_shapes=[dma((3,))],
        compiler_params=pltpu.CompilerParams(vmem_limit_bytes=1000 * 1000),
    )(hidden_grad, gate_grad, weight_grad)
    hidden_grad = hidden_grad.reshape(LOCAL, CAP, NE, HID).transpose(0, 2, 1, 3)[None]
    return hidden_grad, gate_grad.T[None], weight_grad


def solution(mesh):
    return jax.shard_map(
        local,
        mesh=mesh,
        in_specs=(
            P("dp", "ep", None),
            P("dp", "ep", None),
            P("dp", "ep", None),
            P(),
            P("dp", "ep", None, None, None),
            P("dp", "ep"),
        ),
        out_specs=(P("dp", "ep", None, None, None), P("dp", "ep", None), P("dp", "ep")),
        check_vma=False,
    )
```

```python
import jax
import jax.numpy as jnp
from jax import lax
from jax.experimental import pallas as pl
from jax.experimental.pallas import tpu as pltpu
from jax.sharding import PartitionSpec as P

BF = jnp.bfloat16
F32 = jnp.float32
MESH = pl.DeviceIdType.MESH
NX, NY, NC, NZ = 4, 4, 2, 8
NE = NX * NY * NC
TOK, D, TOPK = 128, 2048, 8
EXPERTS, LOCAL, CAP, HID = 128, 4, 12, 768
DS = D // NZ
EXT = D + 2 * EXPERTS
ROWS = CAP * NE


def kernel(
    w_ref, og_ref, rt_ref, gt_ref, es_ref, hs_ref,
    H, gg_ref, O,
    T, W, X, Xf, G, S, Sf, Fst, Tm, Ub, Ur, SG, Pb, meta,
    ag_s, ag_r, rs_s, rs_r, tk_s, tk_r, sb_s, sb_r, sg_s, sg_r, ex_s, ex_r, loc, free,
):
    ep, z = lax.axis_index("ep"), lax.axis_index("dp")
    c, x, y = ep % NC, (ep // NC) % NX, ep // (NC * NX)

    def at(yy, xx, cc):
        return ((yy * NX + xx) * NC + cc, z)

    x_up, x_dn = (x + 1) % NX, (x + NX - 1) % NX
    y_up, y_dn = (y + 1) % NY, (y + NY - 1) % NY
    to_xu, to_xd, to_yu, to_yd = at(y, x_up, c), at(y, x_dn, c), at(y_up, x, c), at(y_dn, x, c)
    sibling = at(y, x, 1 - c)

    turn = (z + NZ + 1 - c) % NZ
    odd, pair = turn % 2, turn // 2
    sign = 2 * odd - 1
    role = [(pair + 1 - odd - sign * j + 8) % LOCAL for j in range(LOCAL)]

    def layer(offset):
        return (z + sign * offset + 2 * NZ) % NZ

    side = [(ep, layer(1)), (ep, layer(-1))]
    partner = side[1]
    way = [1 - odd, odd]

    barrier = pltpu.get_barrier_semaphore()
    for other in (side[0], side[1], to_xu, to_xd, to_yu, to_yd, sibling):
        pl.semaphore_signal(barrier, inc=1, device_id=other, device_id_type=MESH)

    def ag(flow, t, j):
        owner = layer(-t) if flow == 0 else layer(t)
        l = role[j]
        return pltpu.make_async_remote_copy(
            src_ref=w_ref.at[:, pl.ds(pl.multiple_of(l * HID, HID), HID)] if t == 0 else W.at[l, owner],
            dst_ref=W.at[l, owner],
            send_sem=ag_s.at[flow, j, t],
            recv_sem=ag_r.at[way[flow], l, t],
            device_id=side[flow],
            device_id_type=MESH,
        )

    def ag_list(t):
        fwd = [(0, t, j) for j in (0, 1, 2) if t <= 2 * j + 1]
        bwd = [(1, t, j) for j in (3, 2, 1) if t <= 6 - 2 * j]
        both = []
        for i in range(3):
            both += fwd[i : i + 1] + bwd[i : i + 1]
        return both

    def ag_step(t):
        for flow, t, j in ag_list(t):
            if t > 0:
                ag(flow, t - 1, j).wait_recv()
            ag(flow, t, j).start()

    cx = (c, y, x // 2, x % 2)
    own_tokens = pltpu.make_async_copy(og_ref, T.at[(*cx, slice(None), pl.ds(0, D))], loc.at[0])
    own_tokens.start()
    own_saved = pltpu.make_async_copy(hs_ref, H, loc.at[1])
    own_saved.start()
    own_w = [
        pltpu.make_async_copy(w_ref.at[:, pl.ds(l * HID, HID)], W.at[l, z], loc.at[8 + l])
        for l in range(LOCAL)
    ]
    for copy in own_w:
        copy.start()

    io0 = lax.broadcasted_iota(jnp.int32, (EXPERTS, TOK), 0)
    io1 = lax.broadcasted_iota(jnp.int32, (EXPERTS, TOK), 1)
    es = es_ref[...]
    to_slot = (io0 == es).astype(F32).astype(BF)
    slot_of = jnp.transpose(jnp.broadcast_to(es.astype(F32), (EXPERTS, EXPERTS)))
    named = jnp.zeros((EXPERTS, TOK), F32)
    weight = jnp.zeros((EXPERTS, TOK), F32)
    for k in range(TOPK):
        hit = (io0 == rt_ref[k : k + 1, :]).astype(F32)
        named = named + hit
        weight = weight + hit * gt_ref[k : k + 1, :].astype(F32)
        meta[k : k + 1, :] = jnp.sum(hit * slot_of, axis=0, keepdims=True)
    earlier = (io0 < io1).astype(F32).astype(BF)
    rank = jnp.dot(named.astype(BF), earlier, preferred_element_type=F32)
    for k in range(TOPK):
        hit = (io0 == rt_ref[k : k + 1, :]).astype(F32)
        meta[TOPK + k : TOPK + k + 1, :] = jnp.sum(hit * rank, axis=0, keepdims=True)
    ranks = jnp.dot(to_slot, ((rank + 1.0) * named).astype(BF), preferred_element_type=F32)
    gates = jnp.dot(to_slot, weight.astype(BF), preferred_element_type=F32)
    T[c, y, x // 2, x % 2, :, D : D + EXPERTS] = ranks.astype(BF)
    T[c, y, x // 2, x % 2, :, D + EXPERTS : EXT] = jnp.transpose(gates).astype(BF)
    pl.semaphore_wait(barrier, 7)
    ag_step(0)
    own_tokens.wait()

    half = TOK // 2
    up_rows, dn_rows = pl.ds(0, half), pl.ds(half, half)
    quarter = [pl.ds(i * half // 2, half // 2) for i in range(4)]
    every = slice(None)
    x_op, y_op = (x + 2) % NX, (y + 2) % NY

    def blocks(yy, xx, rows):
        if xx is every:
            return T.at[c, yy, :, :, rows]
        if yy is every:
            return T.at[c, :, xx // 2, xx % 2, rows]
        return T.at[c, yy, xx // 2, xx % 2, rows]

    def remote(ref, dst, send, recv, other):
        return pltpu.make_async_remote_copy(
            src_ref=ref, dst_ref=dst, send_sem=send, recv_sem=recv, device_id=other, device_id_type=MESH
        )

    def tk(n, ref, other):
        return remote(ref, ref, tk_s.at[n], tk_r.at[n], other)

    def sb(n, ref):
        return remote(ref, ref, sb_s.at[n], sb_r.at[n], sibling)

    tokens = [
        [
            tk(0, blocks(y, x, up_rows), to_xu),
            tk(1, blocks(y, x, up_rows), to_xd),
            tk(2, blocks(y, x, dn_rows), to_yu),
            tk(3, blocks(y, x, dn_rows), to_yd),
        ],
        [
            tk(4, blocks(y, x_dn, quarter[0]), to_xu),
            tk(5, blocks(y, x_up, quarter[1]), to_xd),
            tk(6, blocks(y_dn, x, quarter[2]), to_yu),
            tk(7, blocks(y_up, x, quarter[3]), to_yd),
        ],
        [
            tk(8, blocks(y, every, up_rows), to_yu),
            tk(9, blocks(y, every, up_rows), to_yd),
            tk(10, blocks(every, x, dn_rows), to_xu),
            tk(11, blocks(every, x, dn_rows), to_xd),
        ],
        [
            tk(12, blocks(y_dn, every, quarter[0]), to_yu),
            tk(13, blocks(y_up, every, quarter[1]), to_yd),
            tk(14, blocks(every, x_dn, quarter[2]), to_xu),
            tk(15, blocks(every, x_up, quarter[3]), to_xd),
        ],
        [],
    ]
    across = [
        [sb(0, blocks(y, x, pl.ds(0, TOK)))],
        [
            sb(1, blocks(y, x_dn, up_rows)),
            sb(2, blocks(y, x_up, up_rows)),
            sb(3, blocks(y_dn, x, dn_rows)),
            sb(4, blocks(y_up, x, dn_rows)),
        ],
        [sb(5, blocks(y, x_op, up_rows)), sb(6, blocks(y_op, x, dn_rows))],
        [
            sb(7, blocks(y_dn, every, up_rows)),
            sb(8, blocks(y_up, every, up_rows)),
            sb(9, blocks(every, x_dn, dn_rows)),
            sb(10, blocks(every, x_up, dn_rows)),
        ],
        [sb(11, blocks(y_op, every, up_rows)), sb(12, blocks(every, x_op, dn_rows))],
    ]

    def phase(n):
        if n > 0:
            for copy in tokens[n - 1]:
                copy.wait_recv()
        for copy in tokens[n] + across[n]:
            copy.start()

    phase(0)
    phase(1)
    phase(2)
    ag_step(1)
    phase(3)
    ag_step(2)
    phase(4)
    own_saved.wait()
    for copies in across:
        for copy in copies:
            copy.wait_recv()

    group = ROWS // 2
    io_row = lax.broadcasted_iota(jnp.int32, (group, TOK), 0).astype(F32)
    io16 = lax.broadcasted_iota(jnp.int32, (16, TOK), 0)
    first = pl.multiple_of((ep // 4) * 16, 16)
    wide = 256

    def pick_rows(ls, a):
        tall = len(ls) * group
        for block in range(16):
            cc, yy, xx = block // 8, (block // 4) % 2, block % 4
            sixteen = T[cc, 2 * a + yy, xx // 2, xx % 2, pl.ds(first, 16), D : D + EXPERTS].astype(F32)
            source = (yy * NX + xx) * NC + cc
            for i, l in enumerate(ls):
                v = jnp.sum(
                    jnp.where(io16 == (ep % 4) * 4 + l, sixteen, 0.0), axis=0, keepdims=True
                )
                v = jnp.where(v > 0.5, 16.0 * v + (source - 16.0), -1.0)
                Pb[i * group : (i + 1) * group, block * TOK : (block + 1) * TOK] = jnp.where(
                    io_row == v, 1.0, 0.0
                ).astype(BF)

        def pick(columns):
            both = [
                jnp.dot(
                    Pb[:tall, cc * 1024 : (cc + 1) * 1024],
                    T[cc, pl.ds(2 * a, 2), :, :, :, columns].reshape(1024, wide),
                    preferred_element_type=F32,
                )
                for cc in range(2)
            ]
            return both[0] + both[1]

        here = pl.ds(a * 16, 16)

        def tile(n, carry):
            columns = pl.ds(pl.multiple_of(n * wide, wide), wide)
            rows = pick(columns).astype(BF)
            for i, l in enumerate(ls):
                X[l, :, here, columns] = rows[i * group : (i + 1) * group].reshape(CAP, 16, wide)
            return carry

        lax.fori_loop(0, D // wide, tile, 0)
        last = pick(slice(D, EXT))
        lane = lax.broadcasted_iota(jnp.int32, (group, wide), 1)
        for i, l in enumerate(ls):
            gate = jnp.sum(
                jnp.where(
                    lane == EXPERTS + ep * LOCAL + l, last[i * group : (i + 1) * group], 0.0
                ),
                axis=1,
                keepdims=True,
            )
            G[l, :, here, :] = jnp.broadcast_to(gate, (group, 128)).reshape(CAP, 16, 128)

    def scale(l):
        gate = G[l].reshape(ROWS, 128)
        for n in range(HID // 128):
            columns = slice(n * 128, (n + 1) * 128)
            S[l, :, columns] = (gate * H[l, :, columns].astype(F32)).astype(BF)

    def half_rows(a):
        here = pl.ds(a * 16, 16)
        return remote(X.at[role[3], :, here], Xf.at[:, here], ex_s.at[3 * a], ex_r.at[3 * a], partner)

    give_rows = [half_rows(0), half_rows(1)]
    give_scaled = remote(S.at[role[3]], Sf, ex_s.at[1], ex_r.at[1], partner)

    pick_rows(role[3:], 0)
    give_rows[0].start()
    pick_rows(role[3:], 1)
    give_rows[1].start()
    scale(role[3])
    give_scaled.start()
    ag_step(3)
    pick_rows(role[:3], 0)
    pick_rows(role[:3], 1)
    for l in role[:3]:
        scale(l)

    for copies in tokens + across:
        for copy in copies:
            copy.wait_send()
    for other in side:
        pl.semaphore_signal(free, inc=1, device_id=other, device_id_type=MESH)

    def landing(l, slot):
        n = l * 9 + slot
        j = n // 3
        columns = pl.ds(pl.multiple_of((n % 3) * HID, HID), HID)
        return (j // 8, (j // 2) % 4, j % 2, slice(None), slice(None), columns)

    def term(j, offset, out, index):
        l, owner = role[j], layer(offset)
        there = pl.ds(pl.multiple_of(owner * DS, DS), DS)
        lhs = X[l, :, :, there].reshape(ROWS, DS)
        other = Xf[:, :, there].reshape(ROWS, DS) if j == 0 else None

        def tile(n, carry):
            columns = pl.ds(pl.multiple_of(n * wide, wide), wide)
            dims = (((0,), (0,)), ((), ()))
            both = lax.dot_general(lhs, S[l, :, columns], dims, preferred_element_type=F32)
            if j == 0:
                both = both + lax.dot_general(
                    other, Sf[:, columns], dims, preferred_element_type=F32
                )
            out[index, :, :, columns] = both.astype(BF).reshape(2, DS // 2, wide)
            return carry

        lax.fori_loop(0, HID // wide, tile, 0)

    def rs(flow, t, j, src):
        slot = 8 - t + 2 * j if flow == 0 else t - 5 + 2 * j
        return remote(
            src,
            T.at[landing(role[j], slot)],
            rs_s.at[flow, j, t],
            rs_r.at[way[flow], role[j], t],
            side[flow],
        )

    def arrived(flow, t, j):
        slot = t - (2 * j - 1) if flow == 0 else 12 - t - 2 * j
        ref = T.at[landing(role[j], slot)]
        remote(ref, ref, rs_s.at[flow, j, t], rs_r.at[way[flow], role[j], t], side[flow]).wait_recv()
        return landing(role[j], slot)

    def reach(flow, t):
        return 6 - t if flow == 0 else t - 6

    def rs_list(t):
        fwd = [(0, j) for j in (2, 1) if t >= 2 * j]
        bwd = [(1, j) for j in (0, 1, 2) if t >= 5 - 2 * j]
        return bwd + fwd if t < 2 else [v for p in zip(fwd + [None] * 3, bwd + [None] * 3) for v in p if v]

    sends = []

    def start(t):
        term(0, 6 - t, Fst, t)
        copy = rs(0, t, 0, Fst.at[t])
        copy.start()
        sends.append(copy)

    def rs_step(t):
        for flow, j in rs_list(t):
            here = arrived(flow, t - 1, j)
            T[here] = (T[here].astype(F32) + Tm[flow * 3 + j].astype(F32)).astype(BF)
            copy = rs(flow, t, j, T.at[here])
            copy.start()
            sends.append(copy)
        for flow, j in rs_list(t):
            if t < 5:
                term(j, reach(flow, t + 1), Tm, flow * 3 + j)

    term(2, reach(1, 1), Tm, 5)
    term(1, reach(0, 2), Tm, 1)
    term(1, reach(1, 3), Tm, 4)
    term(2, reach(0, 4), Tm, 2)
    pl.semaphore_wait(free, 2)
    give_scaled.wait_recv()
    for copy in give_rows:
        copy.wait_recv()
    start(0)
    ag_step(4)
    start(1)

    def u_tile(rows, l, n):
        columns = pl.ds(pl.multiple_of(n * wide, wide), wide)
        weights = W[l, :, :, columns].reshape(D, wide)
        return columns, jnp.dot(rows, weights, preferred_element_type=F32)

    def note(l, slot):
        lane = lax.broadcasted_iota(jnp.int32, (NE, 128), 1)
        mine = SG[c, y, x]
        for s in range(CAP):
            mine = jnp.where(lane == l * 16 + s, slot[s * NE : (s + 1) * NE, :], mine)
        SG[c, y, x] = mine

    def upstream(j, carry):
        l = (pair + 1 - odd - sign * j + 8) % LOCAL
        gate = jnp.concatenate([G[l].reshape(ROWS, 128)] * (wide // 128), axis=1)

        def tile(n, slot):
            columns, u = u_tile(X[l].reshape(ROWS, D), l, n)
            slot = slot + jnp.sum(H[l, :, columns].astype(F32) * u, axis=1, keepdims=True)
            H[l, :, columns] = (gate * u).astype(BF)
            return slot

        note(l, lax.fori_loop(0, HID // wide, tile, jnp.zeros((ROWS, 1), F32)))
        return carry

    def upstream_given():
        def tile(n, carry):
            columns, u = u_tile(Xf[...].reshape(ROWS, D), role[0], n)
            Ub[:, columns] = u.astype(BF)
            return carry

        lax.fori_loop(0, HID // wide, tile, 0)

    def upstream_away():
        l = role[3]
        gate = G[l].reshape(ROWS, 128)
        slot = jnp.zeros((ROWS, 1), F32)
        for n in range(HID // 128):
            columns = slice(n * 128, (n + 1) * 128)
            u = Ur[:, columns].astype(F32)
            slot = slot + jnp.sum(H[l, :, columns].astype(F32) * u, axis=1, keepdims=True)
            H[l, :, columns] = (gate * u).astype(BF)
        note(l, slot)

    give_u = remote(Ub, Ur, ex_s.at[2], ex_r.at[2], partner)

    def sg(n, ref, other):
        return remote(ref, ref, sg_s.at[n], sg_r.at[n], other)

    slots = [
        [sg(0, SG.at[c, y, x], to_xu), sg(1, SG.at[c, y, x], to_xd)],
        [sg(2, SG.at[c, y, x_dn], to_xu)],
        [sg(3, SG.at[c, y], to_yu), sg(4, SG.at[c, y], to_yd)],
        [sg(5, SG.at[c, y_dn], to_yu)],
        [sg(6, SG.at[c], sibling)],
    ]

    def pass_on(n):
        if n > 0:
            for copy in slots[n - 1]:
                copy.wait_recv()
        for copy in slots[n]:
            copy.start()

    SG[c, y, x] = jnp.zeros((NE, 128), F32)

    rs_step(1)
    start(2)
    start(3)
    ag_step(5)
    rs_step(2)
    start(4)
    for t in range(6):
        ag(1, t, 0).wait_recv()
    for copy in own_w:
        copy.wait()
    upstream_given()
    give_u.start()
    rs_step(3)
    start(5)
    upstream(2, 0)
    rs_step(4)
    lax.fori_loop(0, 2, upstream, 0)
    term(0, reach(1, 5), Tm, 3)
    give_u.wait_recv()
    upstream_away()
    pass_on(0)
    rs_step(5)
    pass_on(1)
    for j in range(3):
        term(j, 0, Tm, j)
    pass_on(2)
    pass_on(3)
    pass_on(4)
    slots[4][0].wait_recv()

    row = lax.broadcasted_iota(jnp.int32, (NE, NE, 128), 1)
    by_dev = jnp.sum(jnp.where(row == ep, SG[...].reshape(NE, NE, 128), 0.0), axis=1)
    high = by_dev.astype(BF)
    low = (by_dev - high.astype(F32)).astype(BF)
    io_dev = lax.broadcasted_iota(jnp.int32, (NE, TOK), 0)
    io_in = lax.broadcasted_iota(jnp.int32, (128, TOK), 0)
    for k in range(TOPK):
        q = meta[k : k + 1, :].astype(jnp.int32)
        r = meta[TOPK + k : TOPK + k + 1, :].astype(jnp.int32)
        device = lax.shift_right_logical(q, 2)
        place = lax.bitwise_and(device, 1) * 16 + lax.shift_right_logical(device, 1)
        pickers = (io_dev == place).astype(F32).astype(BF)
        found = sum(
            lax.dot_general(part, pickers, (((0,), (0,)), ((), ())), preferred_element_type=F32)
            for part in (high, low)
        )
        inside = lax.bitwise_and(q, 3) * 16 + r
        gg_ref[k : k + 1, :] = jnp.sum(
            jnp.where(io_in == inside, found, 0.0), axis=0, keepdims=True
        )

    for j, flows in ((3, (0,)), (2, (0, 1)), (1, (0, 1)), (0, (1,))):
        total = Tm[j].astype(F32) if j < 3 else None
        for flow in flows:
            part = T[arrived(flow, 5, j)].astype(F32)
            total = part if total is None else total + part
        l = role[j]
        O[:, pl.ds(pl.multiple_of(l * HID, HID), HID)] = total.reshape(DS, HID)

    for t in range(6):
        for flow, t, j in ag_list(t):
            ag(flow, t, j).wait_send()
    for copy in sends + give_rows + [give_scaled, give_u]:
        copy.wait_send()
    for copies in slots:
        for copy in copies:
            copy.wait_send()


def write(h_ref, g_ref, w_ref, h_out, g_out, w_out, sem):
    pairs = ((w_ref, w_out), (h_ref, h_out), (g_ref, g_out))
    copies = [pltpu.make_async_copy(a, b, sem.at[i]) for i, (a, b) in enumerate(pairs)]
    for copy in copies:
        copy.start()
    for copy in copies:
        copy.wait()


def local(out_grad, gates, routes, expert_slot, hidden_saved, w_down):
    hbm, vmem = pl.BlockSpec(memory_space=pl.ANY), pl.BlockSpec(memory_space=pltpu.VMEM)
    dma = pltpu.SemaphoreType.DMA
    saved = hidden_saved[0].transpose(0, 2, 1, 3).reshape(LOCAL, ROWS, HID)
    hidden_grad, gate_grad, weight_grad = pl.pallas_call(
        kernel,
        out_shape=(
            pltpu.VMEM((LOCAL, ROWS, HID), BF),
            pltpu.VMEM((TOPK, TOK), F32),
            pltpu.VMEM((DS, LOCAL * HID), F32),
        ),
        in_specs=[hbm, hbm, vmem, vmem, vmem, hbm],
        out_specs=(vmem, vmem, vmem),
        scratch_shapes=[
            pltpu.VMEM((NC, NY, NX // 2, 2, TOK, EXT), BF),
            pltpu.VMEM((LOCAL, NZ, DS, HID), BF),
            pltpu.VMEM((LOCAL, CAP, NE, D), BF),
            pltpu.VMEM((CAP, NE, D), BF),
            pltpu.VMEM((LOCAL, CAP, NE, 128), F32),
            pltpu.VMEM((LOCAL, ROWS, HID), BF),
            pltpu.VMEM((ROWS, HID), BF),
            pltpu.VMEM((6, 2, DS // 2, HID), BF),
            pltpu.VMEM((6, 2, DS // 2, HID), BF),
            pltpu.VMEM((ROWS, HID), BF),
            pltpu.VMEM((ROWS, HID), BF),
            pltpu.VMEM((NC, NY, NX, NE, 128), F32),
            pltpu.VMEM((3 * ROWS // 2, 16 * TOK), BF),
            pltpu.VMEM((2 * TOPK, TOK), F32),
            dma((2, LOCAL, 6)),
            dma((2, LOCAL, 6)),
            dma((2, LOCAL, 6)),
            dma((2, LOCAL, 6)),
            dma((16,)),
            dma((16,)),
            dma((13,)),
            dma((13,)),
            dma((7,)),
            dma((7,)),
            dma((4,)),
            dma((4,)),
            dma((12,)),
            pltpu.SemaphoreType.REGULAR,
        ],
        compiler_params=pltpu.CompilerParams(
            collective_id=0, has_side_effects=True, vmem_limit_bytes=57 * 1000 * 1000
        ),
        cost_estimate=pl.CostEstimate(
            flops=20_000_000_000, bytes_accessed=15_000_000, transcendentals=0
        ),
    )(
        w_down,
        out_grad[0],
        routes[0].T,
        gates[0].T,
        expert_slot.reshape(1, EXPERTS),
        saved,
    )
    hidden_grad, gate_grad, weight_grad = pl.pallas_call(
        write,
        out_shape=(
            jax.ShapeDtypeStruct((LOCAL, ROWS, HID), BF),
            jax.ShapeDtypeStruct((TOPK, TOK), F32),
            jax.ShapeDtypeStruct((DS, LOCAL * HID), F32),
        ),
        in_specs=[vmem, vmem, vmem],
        out_specs=(hbm, hbm, hbm),
        scratch_shapes=[dma((3,))],
        compiler_params=pltpu.CompilerParams(vmem_limit_bytes=1000 * 1000),
    )(hidden_grad, gate_grad, weight_grad)
    hidden_grad = hidden_grad.reshape(LOCAL, CAP, NE, HID).transpose(0, 2, 1, 3)[None]
    return hidden_grad, gate_grad.T[None], weight_grad


def solution(mesh):
    return jax.shard_map(
        local,
        mesh=mesh,
        in_specs=(
            P("dp", "ep", None),
            P("dp", "ep", None),
            P("dp", "ep", None),
            P(),
            P("dp", "ep", None, None, None),
            P("dp", "ep"),
        ),
        out_specs=(P("dp", "ep", None, None, None), P("dp", "ep", None), P("dp", "ep")),
        check_vma=False,
    )
```
